32 devices in a mesh: heads: 1, ctx: 32 (over z, y, x, core).
Axes of the slice: x: 2, y: 2, z: 4, core: 2. Of those that a mesh axis runs over, the one named last changes fastest.
Arguments:
- hidden: bfloat16 [4096, 4096], P('ctx', 'heads'), may hold values from -6 to 6
- w_query: bfloat16 [4096, 1024], P('ctx', 'heads'), may hold values from -0.09375 to 0.09375
- key_input: bfloat16 [4096, 1024], P('ctx', 'heads'), may hold values from -6 to 6
- values: bfloat16 [4096, 512], P('ctx', 'heads'), may hold values from -6 to 6
- cotangent: bfloat16 [4096, 512], P('ctx', 'heads'), may hold values from -6 to 6
Outputs:
- attended: bfloat16 [4096, 512], P('ctx', 'heads')
- query_grad: float32 [4096, 1024], P('ctx', 'heads')
- key_grad: bfloat16 [4096, 1024], P('ctx', 'heads')
- value_grad: bfloat16 [4096, 512], P('ctx', 'heads')
The draws below stay inside these ranges and needn't reach their ends.
All inputs are finite; a program needn't handle non-finite values.
Results may differ from the reference program's by a relative error of at most 0.015.
Values may be sent and summed in bfloat16 or wider, within the bound.
No kernel may reach another device: no remote copies, remote signals or barrier semaphores. Data moves between devices by JAX's collectives and lax.ppermute only.
A program may use at most 128 MiB of HBM per device.

```python
import jax
import jax.numpy as jnp
from jax import lax

D = 4096
HEAD_DIM = 128
FEAT = 256
HEADS_GROUP = 4
TOK_DEV = 128
HEADS = 4
LENGTH = 4096
N_HEADS = 1


def levels(own_key, extent, cuts, low, largest):
    level, own = 1.0, jax.random.fold_in(own_key, 6)
    for axis_at, blocks in cuts:
        heights = jnp.exp(jax.random.uniform(jax.random.fold_in(own, axis_at), (blocks,), jnp.float32, low / len(cuts), largest / len(cuts)))
        level = level * jnp.repeat(heights, extent[axis_at] // blocks).reshape([-1 if axis == axis_at else 1 for axis in range(len(extent))])
    return level


def normal_values(rng, dims, width, reach, pieces=(), held_as=jnp.bfloat16):
    array = width * jax.random.normal(rng, dims, jnp.float32)
    if pieces:
        array = array * levels(rng, dims, pieces, -0.22, 0.18)
    return jnp.clip(array, -reach, reach).astype(held_as)


def setup_inputs(seed: int = 0) -> dict:
    seeds = jax.random.split(jax.random.key(seed), 6)
    return {
        "hidden": normal_values(seeds[0], (LENGTH, D), 1.0, 6.0, ((0, 32),)),
        "w_query": normal_values(seeds[1], (D, HEADS * FEAT), D ** -0.5, 0.09375, ((0, 32),)),
        "key_input": normal_values(seeds[2], (LENGTH, HEADS * FEAT), 1.0, 6.0, ((0, 32),)),
        "values": normal_values(seeds[3], (LENGTH, HEADS * HEAD_DIM), 1.0, 6.0, ((0, 32),)),
        "cotangent": normal_values(seeds[4], (LENGTH, HEADS * HEAD_DIM), 1.0, 6.0, ((0, 32),)),
    }


EPSILON = 1e-06
HIGHEST = lax.Precision.HIGHEST

def reference(hidden, w_query, key_input, values, cotangent):
    head_count = HEADS_GROUP * N_HEADS
    length = hidden.shape[0]
    blocks = length // TOK_DEV
    query_proj = jnp.dot(hidden, w_query, preferred_element_type=jnp.float32)
    query_feats = jnp.maximum(query_proj, 0.0).astype(jnp.bfloat16)
    key_feats = jnp.maximum(key_input, jnp.zeros_like(key_input))
    causal = jnp.arange(TOK_DEV)[:, None] >= jnp.arange(TOK_DEV)[None, :]
    block_queries = query_feats.reshape(blocks, TOK_DEV, head_count, FEAT)
    block_keys = key_feats.reshape(blocks, TOK_DEV, head_count, FEAT)
    block_values = values.reshape(blocks, TOK_DEV, head_count, HEAD_DIM)

    def make_scores(queries, keys_here):
        raw = jnp.einsum('thf,shf->hts', queries.astype(jnp.float32), keys_here.astype(jnp.float32))
        return jnp.where(causal[None], raw, 0.0).astype(jnp.bfloat16)

    def forward(carried, block_data):
        queries, keys_here, value_rows = block_data
        scores = make_scores(queries, keys_here)
        inner = jnp.einsum('hts,she->the', scores.astype(jnp.float32), value_rows.astype(jnp.float32))
        outer = jnp.einsum('thf,hfe->the', queries.astype(jnp.float32), carried, precision=HIGHEST)
        update = jnp.einsum('shf,she->hfe', keys_here.astype(jnp.float32), value_rows.astype(jnp.float32))
        return (carried + update, (inner + outer, carried))
    empty = jnp.zeros((head_count, FEAT, HEAD_DIM), jnp.float32)
    unused, (numerators, priors) = lax.scan(forward, empty, (block_queries, block_keys, block_values))
    numerator = numerators.reshape(length, head_count, HEAD_DIM)
    inv_rms = lax.rsqrt(lax.optimization_barrier(jnp.mean(numerator * numerator, axis=-1, keepdims=True)) + EPSILON)
    normed = numerator * inv_rms
    attended = normed.astype(jnp.bfloat16).reshape(length, head_count * HEAD_DIM)
    grad_out = cotangent.astype(jnp.float32).reshape(length, head_count, HEAD_DIM)
    d_numer = (inv_rms * (grad_out - normed * lax.optimization_barrier(jnp.mean(grad_out * normed, axis=-1, keepdims=True)))).astype(jnp.bfloat16)
    block_dnum = d_numer.reshape(blocks, TOK_DEV, head_count, HEAD_DIM)

    def backward(carried, block_data):
        queries, keys_here, value_rows, dnum_rows, prior_state = block_data
        scores = make_scores(queries, keys_here).astype(jnp.float32)
        queries32 = queries.astype(jnp.float32)
        keys32 = keys_here.astype(jnp.float32)
        values32 = value_rows.astype(jnp.float32)
        dnum32 = dnum_rows.astype(jnp.float32)
        mixed_raw = jnp.einsum('the,she->hts', dnum32, values32)
        mixed_scores = jnp.where(causal[None], mixed_raw, 0.0).astype(jnp.bfloat16).astype(jnp.float32)
        d_featq = jnp.einsum('hts,shf->thf', mixed_scores, keys32) + jnp.einsum('the,hfe->thf', dnum32, prior_state, precision=HIGHEST)
        d_vals = jnp.einsum('hts,the->she', scores, dnum32) + jnp.einsum('shf,hfe->she', keys32, carried, precision=HIGHEST)
        d_featk = jnp.einsum('hts,thf->shf', mixed_scores, queries32) + jnp.einsum('she,hfe->shf', values32, carried, precision=HIGHEST)
        update = jnp.einsum('thf,the->hfe', queries32, dnum32)
        return (carried + update, (d_featq, d_vals, d_featk))
    unused_two, (d_featq, d_vals, d_featk) = lax.scan(backward, empty, (block_queries, block_keys, block_values, block_dnum, priors), reverse=True)
    d_query = jnp.where(query_proj > 0, d_featq.reshape(length, head_count * FEAT), 0.0).astype(jnp.bfloat16)
    query_grad = lax.dot_general(hidden, d_query, (((0,), (0,)), ((), ())), preferred_element_type=jnp.float32)
    value_grad = d_vals.reshape(length, head_count * HEAD_DIM).astype(jnp.bfloat16)
    key_grad = jnp.where(key_input > 0, d_featk.reshape(length, head_count * FEAT), 0.0).astype(jnp.bfloat16)
    return (attended, query_grad, key_grad, value_grad)
```

```python
import functools

import jax
import jax.numpy as jnp
from jax import lax
from jax.experimental import pallas as pl
from jax.experimental.pallas import tpu as pltpu
from jax.sharding import PartitionSpec as P

HEAD_DIM = 128
FEAT = 256
HEADS_GROUP = 4
CORES = 2
EPSILON = 1e-06

F32 = jnp.float32
BF16 = jnp.bfloat16
HALF = FEAT // 2


def dot(a, b, dims=((1,), (0,))):
    return lax.dot_general(a, b, (dims, ((), ())), preferred_element_type=F32)


def split(x):
    high = x.astype(BF16)
    return high, (x - high.astype(F32)).astype(BF16)


def call(kernel, outs, args, flops=0, scratch=(), mib=48):
    shapes = [jax.ShapeDtypeStruct(shape, dtype) for shape, dtype in outs]
    moved = sum(a.size * a.dtype.itemsize for a in args) + sum(s.size * s.dtype.itemsize for s in shapes)
    return pl.pallas_call(
        kernel,
        out_shape=shapes,
        in_specs=[pl.BlockSpec(memory_space=pltpu.SMEM)]
        + [pl.BlockSpec(memory_space=pltpu.VMEM)] * (len(args) - 1),
        out_specs=[pl.BlockSpec(memory_space=pltpu.VMEM)] * len(shapes),
        scratch_shapes=list(scratch),
        compiler_params=pltpu.CompilerParams(vmem_limit_bytes=mib << 20),
        cost_estimate=pl.CostEstimate(flops=flops, bytes_accessed=moved, transcendentals=0),
    )(*args)


def lanes(index, width):
    return pl.ds(pl.multiple_of(index * width, width), width)


def pack_kernel(place, w, key, val, cot, *outs):
    rows, depth = key.shape[0], w.shape[0]
    for k, out in enumerate(outs):
        head = place[0] ^ k
        out[:depth, :] = w[:, lanes(head, FEAT)]
        out[depth : depth + rows, :] = key[:, lanes(head, FEAT)]
        out[depth + rows :, :HEAD_DIM] = val[:, lanes(head, HEAD_DIM)]
        out[depth + rows :, HEAD_DIM:] = cot[:, lanes(head, HEAD_DIM)]


def state_kernel(rows, depth, place, p0, p1, p2, p3, pay, states):
    total = jnp.zeros((FEAT, HEAD_DIM), F32)
    for j, p in enumerate((p0, p1, p2, p3)):
        pay[j * depth : (j + 1) * depth, :] = p[:depth, :]
        keys = jnp.maximum(p[depth : depth + rows, :], 0)
        state = dot(keys, p[depth + rows :, :HEAD_DIM], ((0,), (0,)))
        states[j] = state.astype(BF16)
        total = total + state
    total = total.astype(BF16)
    pay[4 * depth :, :HEAD_DIM] = total[:HALF, :]
    pay[4 * depth :, HEAD_DIM:] = total[HALF:, :]


def hidden_columns(h, start, width):
    cols = pl.ds(start, width)
    return jnp.concatenate([ref[:, cols] for ref in h], axis=0)


def attend_kernel(rows, depth, outer, place, *refs):
    h, refs = refs[:7], refs[7:]
    p, refs = refs[:4], refs[4:]
    own_pay, refs = refs[:outer], refs[outer:]
    other_pay, refs = refs[:outer], refs[outer:]
    own_states, other_states, att, dq_t, grown, grown_sum, val_part, key_part, weights, proj = refs
    q, z, core = place[0], place[1], place[2]
    base = jnp.zeros((FEAT, HEAD_DIM), F32)
    for k in range(outer):
        for flip, pay in ((0, own_pay[k]), (1, other_pay[k])):
            for j in range(4):
                at = (((z ^ k) * 4 + (q ^ j)) * CORES + (core ^ flip)) * depth
                weights[pl.ds(pl.multiple_of(at, depth), depth), :] = pay[j * depth : (j + 1) * depth, :]
            if k:
                seen = ((z ^ k) < z).astype(jnp.int32).astype(F32)
                packed = pay[4 * depth :, :].astype(F32)
                base = base + seen * jnp.concatenate([packed[:, :HEAD_DIM], packed[:, HEAD_DIM:]], axis=0)
    width = h[0].shape[1]
    step = min(512, width)
    for at in range(0, width, step):
        part = dot(hidden_columns(h, at, step), weights[at : at + step, :])
        if at:
            proj[...] += part
        else:
            proj[...] = part
    own = [own_states[j].astype(F32) for j in range(4)]
    other = [other_states[j].astype(F32) for j in range(4)]
    causal = lax.broadcasted_iota(jnp.int32, (rows, rows), 0) >= lax.broadcasted_iota(
        jnp.int32, (rows, rows), 1
    )
    total = jnp.zeros((FEAT, HEAD_DIM), F32)
    for j in range(4):
        here = (q ^ j) * CORES + core
        prior = base
        for i in range(4):
            for flip, group in ((0, own), (1, other)):
                if flip == 0 and i == j:
                    continue
                there = (q ^ i) * CORES + (core ^ flip)
                prior = prior + (there < here).astype(jnp.int32).astype(F32) * group[i]
        prior_high, prior_low = split(prior)
        block = slice(j * rows, (j + 1) * rows)
        query = proj[block, :]
        feats = jnp.maximum(query, 0.0).astype(BF16)
        keys = jnp.maximum(p[j][depth : depth + rows, :], 0)
        vals = p[j][depth + rows :, :HEAD_DIM]
        grad = p[j][depth + rows :, HEAD_DIM:].astype(F32)
        scores = jnp.where(causal, dot(feats, keys, ((1,), (1,))), 0.0).astype(BF16)
        numer = dot(scores, vals) + dot(feats, prior_high) + dot(feats, prior_low)
        inv = lax.rsqrt(jnp.mean(numer * numer, axis=-1, keepdims=True) + EPSILON)
        normed = numer * inv
        att[j] = normed.astype(BF16)
        d_num = (inv * (grad - normed * jnp.mean(grad * normed, axis=-1, keepdims=True))).astype(BF16)
        mixed = jnp.where(causal, dot(d_num, vals, ((1,), (1,))), 0.0).astype(BF16)
        d_feat = dot(mixed, keys) + dot(d_num, prior_high, ((1,), (1,))) + dot(d_num, prior_low, ((1,), (1,)))
        d_query = jnp.where(query > 0, d_feat, 0.0)
        dq_t[:, block] = d_query.T.astype(BF16)
        grown_j = dot(feats, d_num, ((0,), (0,)))
        grown[j] = grown_j.astype(BF16)
        total = total + grown_j
        val_part[block, :] = dot(scores, d_num, ((0,), (0,)))
        key_part[block, :] = dot(mixed, feats, ((0,), (0,)))
    grown_sum[...] = total.astype(BF16)


def grad_kernel(depth, outer, place, *refs):
    h, dq_t, keep, give = refs[:7], refs[7], refs[8], refs[9:]
    z, core = place[1], place[2]
    pair = CORES * depth
    lhs = dq_t[...]
    for k in range(outer):
        for i in range(4):
            start = pl.multiple_of(((z ^ k) * 4 + i) * pair, pair)
            out = dot(lhs, hidden_columns(h, start, pair))
            even, odd = out[:, :depth], out[:, depth:]
            first = jnp.broadcast_to(core == 0, even.shape)
            keep[k, :, i * depth : (i + 1) * depth] = jnp.where(first, even, odd)
            give[k][:, i * depth : (i + 1) * depth] = jnp.where(first, odd, even).astype(BF16)


def add_kernel(outer, place, keep, *refs):
    gifts, own, outs = refs[:outer], refs[outer], refs[outer + 1 :]
    for k in range(outer):
        total = keep[k] + gifts[k][...].astype(F32)
        if k:
            outs[k - 1][...] = total.astype(BF16)
        else:
            own[...] = total


def sum_kernel(depth, place, own, *refs):
    arrived, (mine, *outs), blocks = refs[:-5], refs[-5:-1], refs[-1]
    total = own[...]
    for ref in arrived:
        total = total + ref[...].astype(F32)
    for i in range(4):
        blocks[place[0] ^ i] = total[:, i * depth : (i + 1) * depth]
    mine[...] = blocks[0]
    for k, out in enumerate(outs):
        out[...] = blocks[k + 1].astype(BF16)


def query_grad_kernel(place, *refs):
    out = refs[-1]
    for k, ref in enumerate(refs[:-1]):
        out[:, lanes(place[0] ^ k, FEAT)] = ref[...].astype(F32).T


def finish_kernel(rows, depth, outer, place, *refs):
    p, refs = refs[:4], refs[4:]
    att, val_part, key_part, own_grown, other_grown, own_rest, other_rest, *outs = refs
    q, core = place[0], place[2]
    base = own_rest[...].astype(F32) + other_rest[...].astype(F32)
    own = [own_grown[j].astype(F32) for j in range(4)]
    other = [other_grown[j].astype(F32) for j in range(4)]
    for j, out in enumerate(outs):
        here = (q ^ j) * CORES + core
        later = base
        for i in range(4):
            for flip, group in ((0, own), (1, other)):
                if flip == 0 and i == j:
                    continue
                there = (q ^ i) * CORES + (core ^ flip)
                later = later + (there > here).astype(jnp.int32).astype(F32) * group[i]
        high, low = split(later)
        block = slice(j * rows, (j + 1) * rows)
        raw = p[j][depth : depth + rows, :]
        keys = jnp.maximum(raw, 0)
        vals = p[j][depth + rows :, :HEAD_DIM]
        d_val = val_part[block, :] + dot(keys, high) + dot(keys, low)
        d_key = key_part[block, :] + dot(vals, high, ((1,), (1,))) + dot(vals, low, ((1,), (1,)))
        out[:, :HEAD_DIM] = att[j]
        out[:, HEAD_DIM : 2 * HEAD_DIM] = d_val.astype(BF16)
        out[:, 2 * HEAD_DIM :] = jnp.where(raw.astype(F32) > 0, d_key, 0.0).astype(BF16)


def place_kernel(place, *refs):
    att, key_grad, val_grad = refs[-3:]
    for k, ref in enumerate(refs[:-3]):
        head = place[0] ^ k
        att[:, lanes(head, HEAD_DIM)] = ref[:, :HEAD_DIM]
        val_grad[:, lanes(head, HEAD_DIM)] = ref[:, HEAD_DIM : 2 * HEAD_DIM]
        key_grad[:, lanes(head, FEAT)] = ref[:, 2 * HEAD_DIM :]


def body(hidden, w_query, key_input, values, cotangent):
    count = lax.axis_size("ctx")
    me = lax.axis_index("ctx")
    inner = CORES * HEADS_GROUP
    outer = count // inner
    rows, depth = key_input.shape[0], w_query.shape[0]
    if lax.axis_size("heads") > 1:
        hidden = lax.all_gather(hidden, "heads", axis=1, tiled=True)
    width = hidden.shape[1]
    place = jnp.stack([me // CORES % HEADS_GROUP, me // inner, me % CORES]).astype(jnp.int32)

    def swap(block, bits):
        return lax.ppermute(block, "ctx", [(i, i ^ bits) for i in range(count)])

    def core_swap(block):
        return swap(block, 1)

    def chip_swap(block, k):
        return swap(block, CORES * k)

    def plane_swap(block, k):
        return swap(block, inner * k)

    def down(block, k):
        return lax.ppermute(block, "ctx", [(i, i - inner * k) for i in range(inner * k, count)])

    packs = call(
        pack_kernel,
        [((depth + 2 * rows, FEAT), BF16)] * 4,
        [place, w_query, key_input, values, cotangent],
    )
    p = [packs[0]] + [chip_swap(packs[k], k) for k in (1, 2, 3)]
    top, bottom = hidden[: rows // 2], hidden[rows // 2 :]
    h1t = chip_swap(top, 1)
    h2b = chip_swap(bottom, 2)
    h3t = chip_swap(h1t, 2)
    h3b = chip_swap(h2b, 1)
    h1b = chip_swap(bottom, 1)
    h2t = chip_swap(top, 2)
    h = [hidden, h1t, h1b, h2t, h2b, h3t, h3b]
    pay, states = call(
        functools.partial(state_kernel, rows, depth),
        [((4 * depth + HALF, FEAT), BF16), ((4, FEAT, HEAD_DIM), BF16)],
        [place, *p],
        flops=2 * 4 * rows * FEAT * HEAD_DIM,
    )
    pays = [pay] + [None] * (outer - 1)
    for k in reversed(range(1, outer)):
        pays[k] = plane_swap(pay, k)
    other_pays = [core_swap(pays[k]) for k in range(outer)]
    other_states = core_swap(states)
    positions = 4 * rows
    att, dq_t, grown, grown_sum, val_part, key_part = call(
        functools.partial(attend_kernel, rows, depth, outer),
        [
            ((4, rows, HEAD_DIM), BF16),
            ((FEAT, positions), BF16),
            ((4, FEAT, HEAD_DIM), BF16),
            ((FEAT, HEAD_DIM), BF16),
            ((positions, HEAD_DIM), F32),
            ((positions, FEAT), F32),
        ],
        [place, *h, *p, *pays, *other_pays, states, other_states],
        flops=2 * positions * width * FEAT + 24 * positions * FEAT * HEAD_DIM,
        scratch=[pltpu.VMEM((width, FEAT), BF16), pltpu.VMEM((positions, FEAT), F32)],
    )
    other_grown = core_swap(grown)
    later = [down(grown_sum, k) for k in range(1, outer)]
    keep, *give = call(
        functools.partial(grad_kernel, depth, outer),
        [((outer, FEAT, 4 * depth), F32)] + [((FEAT, 4 * depth), BF16)] * outer,
        [place, *h, dq_t],
        flops=2 * positions * width * FEAT,
    )
    gifts = [core_swap(g) for g in give]
    own, *sent = call(
        functools.partial(add_kernel, outer),
        [((FEAT, 4 * depth), F32)] + [((FEAT, 4 * depth), BF16)] * (outer - 1),
        [place, keep, *gifts],
    )
    arrived = [plane_swap(sent[k - 1], k) for k in reversed(range(1, outer))]
    rest = sum((x.astype(F32) for x in later), jnp.zeros((FEAT, HEAD_DIM), F32)).astype(BF16)
    other_rest = core_swap(rest)
    outs = call(
        functools.partial(finish_kernel, rows, depth, outer),
        [((rows, 2 * HEAD_DIM + FEAT), BF16)] * 4,
        [place, *p, att, val_part, key_part, grown, other_grown, rest, other_rest],
        flops=16 * positions * FEAT * HEAD_DIM,
    )
    placed = [outs[0]] + [chip_swap(outs[k], k) for k in (1, 2, 3)]
    attended, key_grad, value_grad = call(
        place_kernel,
        [
            ((rows, HEADS_GROUP * HEAD_DIM), BF16),
            ((rows, HEADS_GROUP * FEAT), BF16),
            ((rows, HEADS_GROUP * HEAD_DIM), BF16),
        ],
        [place, *placed],
    )
    blocks = call(
        functools.partial(sum_kernel, depth),
        [((FEAT, depth), F32)] + [((FEAT, depth), BF16)] * 3,
        [place, own, *arrived],
        scratch=[pltpu.VMEM((4, FEAT, depth), F32)],
    )
    columns = [blocks[0]] + [chip_swap(blocks[k], k) for k in (1, 2, 3)]
    (query_grad,) = call(
        query_grad_kernel, [((depth, HEADS_GROUP * FEAT), F32)], [place, *columns]
    )
    return (attended, query_grad, key_grad, value_grad)


def solution(mesh):
    return jax.shard_map(
        body,
        mesh=mesh,
        in_specs=(P("ctx", "heads"),) * 5,
        out_specs=(P("ctx", "heads"),) * 4,
        check_vma=False,
    )
```

```python
import functools

import jax
import jax.numpy as jnp
from jax import lax
from jax.experimental import pallas as pl
from jax.experimental.pallas import tpu as pltpu
from jax.sharding import PartitionSpec as P

HEAD_DIM = 128
FEAT = 256
HEADS_GROUP = 4
CORES = 2
EPSILON = 1e-06

F32 = jnp.float32
BF16 = jnp.bfloat16
HALF = FEAT // 2
URGENT = 1 << 35


def dot(a, b, dims=((1,), (0,))):
    return lax.dot_general(a, b, (dims, ((), ())), preferred_element_type=F32)


def split(x):
    high = x.astype(BF16)
    return high, (x - high.astype(F32)).astype(BF16)


def seat(place):
    me = place[0]
    low, high = CORES.bit_length() - 1, (CORES * HEADS_GROUP).bit_length() - 1
    return me >> low & HEADS_GROUP - 1, me >> high, me & CORES - 1


def call(kernel, outs, args, flops=0, scratch=(), mib=16, space=pltpu.VMEM, urgent=False):
    shapes = [jax.ShapeDtypeStruct(shape, dtype) for shape, dtype in outs]
    moved = sum(a.size * a.dtype.itemsize for a in args) + sum(s.size * s.dtype.itemsize for s in shapes)
    return pl.pallas_call(
        kernel,
        out_shape=shapes,
        in_specs=[pl.BlockSpec(memory_space=pltpu.SMEM)]
        + [pl.BlockSpec(memory_space=space)] * (len(args) - 1),
        out_specs=[pl.BlockSpec(memory_space=pltpu.VMEM)] * len(shapes),
        scratch_shapes=list(scratch),
        compiler_params=pltpu.CompilerParams(vmem_limit_bytes=mib << 20),
        cost_estimate=pl.CostEstimate(flops=URGENT if urgent else flops, bytes_accessed=moved, transcendentals=0),
    )(*args)


def lanes(index, width):
    return pl.ds(pl.multiple_of(index * width, width), width)


def pack_kernel(place, w, key, val, cot, *refs):
    outs, sems = refs[:4], refs[4]
    rows, depth = key.shape[0], w.shape[0]
    q, _, _ = seat(place)
    copies = []
    for k in (3, 1, 2, 0):
        head, out = q ^ k, outs[k]
        low, high = pl.ds(depth, rows), pl.ds(depth + rows, rows)
        moves = (
            (w.at[:, lanes(head, FEAT)], out.at[pl.ds(0, depth), :]),
            (key.at[:, lanes(head, FEAT)], out.at[low, :]),
            (val.at[:, lanes(head, HEAD_DIM)], out.at[high, pl.ds(0, HEAD_DIM)]),
            (cot.at[:, lanes(head, HEAD_DIM)], out.at[high, pl.ds(HEAD_DIM, HEAD_DIM)]),
        )
        for source, target in moves:
            copies.append(pltpu.make_async_copy(source, target, sems.at[len(copies)]))
            copies[-1].start()
    for copy in copies:
        copy.wait()


def state_kernel(rows, depth, place, p0, p1, p2, p3, pay, states):
    total = jnp.zeros((FEAT, HEAD_DIM), F32)
    for j, p in enumerate((p0, p1, p2, p3)):
        pay[j * depth : (j + 1) * depth, :] = p[:depth, :]
        keys = jnp.maximum(p[depth : depth + rows, :], 0)
        state = dot(keys, p[depth + rows :, :HEAD_DIM], ((0,), (0,)))
        states[j] = state.astype(BF16)
        total = total + state
    total = total.astype(BF16)
    pay[4 * depth :, :HEAD_DIM] = total[:HALF, :]
    pay[4 * depth :, HEAD_DIM:] = total[HALF:, :]


def hidden_columns(h, start, width):
    cols = pl.ds(start, width)
    return jnp.concatenate([ref[:, cols] for ref in h], axis=0)


def before(there, here):
    return (there < here).astype(jnp.int32).astype(F32)


def attend_kernel(rows, depth, outer, place, *refs):
    h, refs = refs[:5], refs[5:]
    p, refs = refs[:4], refs[4:]
    own_pay, refs = refs[:outer], refs[outer:]
    other_pay, refs = refs[:outer], refs[outer:]
    own_states, other_states, att, dq_t, grown, feats_out, d_num_out, scores_out, mixed_out, weights, proj = refs
    q, z, core = seat(place)
    base = jnp.zeros((FEAT, HEAD_DIM), F32)
    for k in range(outer):
        for flip, pay in ((0, own_pay[k]), (1, other_pay[k])):
            for j in range(4):
                at = (((z ^ k) * 4 + (q ^ j)) * CORES + (core ^ flip)) * depth
                weights[pl.ds(pl.multiple_of(at, depth), depth), :] = pay[j * depth : (j + 1) * depth, :]
            if k:
                packed = pay[4 * depth :, :].astype(F32)
                base = base + before(z ^ k, z) * jnp.concatenate(
                    [packed[:, :HEAD_DIM], packed[:, HEAD_DIM:]], axis=0
                )
    width = h[0].shape[1]
    step = min(512, width)
    for at in range(0, width, step):
        part = dot(hidden_columns(h, at, step), weights[at : at + step, :])
        if at:
            proj[...] += part
        else:
            proj[...] = part
    own = [own_states[j].astype(F32) for j in range(4)]
    other = [other_states[j].astype(F32) for j in range(4)]
    causal = lax.broadcasted_iota(jnp.int32, (rows, rows), 0) >= lax.broadcasted_iota(
        jnp.int32, (rows, rows), 1
    )
    for j in range(4):
        here = (q ^ j) * CORES + core
        prior = base
        for i in range(4):
            for flip, group in ((0, own), (1, other)):
                if flip == 0 and i == j:
                    continue
                prior = prior + before((q ^ i) * CORES + (core ^ flip), here) * group[i]
        prior_high, prior_low = split(prior)
        block = slice(j * rows, (j + 1) * rows)
        query = proj[block, :]
        feats = jnp.maximum(query, 0.0).astype(BF16)
        keys = jnp.maximum(p[j][depth : depth + rows, :], 0)
        vals = p[j][depth + rows :, :HEAD_DIM]
        grad = p[j][depth + rows :, HEAD_DIM:].astype(F32)
        scores = jnp.where(causal, dot(feats, keys, ((1,), (1,))), 0.0).astype(BF16)
        numer = dot(scores, vals) + dot(feats, prior_high) + dot(feats, prior_low)
        inv = lax.rsqrt(jnp.mean(numer * numer, axis=-1, keepdims=True) + EPSILON)
        normed = numer * inv
        att[j] = normed.astype(BF16)
        d_num = (inv * (grad - normed * jnp.mean(grad * normed, axis=-1, keepdims=True))).astype(BF16)
        mixed = jnp.where(causal, dot(d_num, vals, ((1,), (1,))), 0.0).astype(BF16)
        d_feat = dot(mixed, keys) + dot(d_num, prior_high, ((1,), (1,))) + dot(d_num, prior_low, ((1,), (1,)))
        d_query = jnp.where(query > 0, d_feat, 0.0)
        dq_t[:, block] = d_query.T.astype(BF16)
        grown[j] = dot(feats, d_num, ((0,), (0,))).astype(BF16)
        feats_out[j] = feats
        d_num_out[j] = d_num
        scores_out[j] = scores
        mixed_out[j] = mixed


def half_kernel(place, own, other, half, total):
    _, _, core = seat(place)
    total[...] = sum(ref[j].astype(F32) for ref in (own, other) for j in range(4))
    half[...] = total[pl.ds(pl.multiple_of(core * HALF, HALF), HALF), :].astype(BF16)


def side_kernel(rows, place, feats, d_num, scores, mixed, val_part, key_part):
    for j in range(4):
        block = slice(j * rows, (j + 1) * rows)
        val_part[block, :] = dot(scores[j], d_num[j], ((0,), (0,)))
        key_part[block, :] = dot(mixed[j], feats[j], ((0,), (0,)))


def grad_kernel(depth, k, place, *refs):
    *h, dq_t, keep, give = refs
    _, z, core = seat(place)
    pair = CORES * depth
    lhs = dq_t[...]
    for i in range(4):
        start = pl.multiple_of(((z ^ k) * 4 + i) * pair, pair)
        out = dot(lhs, hidden_columns(h, start, pair))
        even, odd = out[:, :depth], out[:, depth:]
        first = jnp.broadcast_to(core == 0, even.shape)
        keep[:, i * depth : (i + 1) * depth] = jnp.where(first, even, odd)
        give[:, i * depth : (i + 1) * depth] = jnp.where(first, odd, even).astype(BF16)


def sum_kernel(depth, place, own, *refs):
    arrived, (mine, *outs), blocks = refs[:-5], refs[-5:-1], refs[-1]
    total = own[...]
    for ref in arrived:
        total = total + ref[...].astype(F32)
    q, _, _ = seat(place)
    for i in range(4):
        blocks[q ^ i] = total[:, i * depth : (i + 1) * depth]
    mine[...] = blocks[0]
    for k, out in enumerate(outs):
        out[...] = blocks[k + 1].astype(BF16)


def query_grad_kernel(place, *refs):
    out = refs[-1]
    q, _, _ = seat(place)
    for k, ref in enumerate(refs[:-1]):
        out[:, lanes(q ^ k, FEAT)] = ref[...].astype(F32).T


def finish_kernel(rows, depth, outer, place, *refs):
    p, refs = refs[:4], refs[4:]
    att, val_part, key_part, own_grown, other_grown, own_rest, other_rest, *outs, rest = refs
    q, _, core = seat(place)
    for flip, ref in ((0, own_rest), (1, other_rest)):
        rest[pl.ds(pl.multiple_of((core ^ flip) * HALF, HALF), HALF), :] = ref[...].astype(F32)
    base = rest[...]
    own = [own_grown[j].astype(F32) for j in range(4)]
    other = [other_grown[j].astype(F32) for j in range(4)]
    for j, out in enumerate(outs):
        here = (q ^ j) * CORES + core
        later = base
        for i in range(4):
            for flip, group in ((0, own), (1, other)):
                if flip == 0 and i == j:
                    continue
                later = later + before(here, (q ^ i) * CORES + (core ^ flip)) * group[i]
        high, low = split(later)
        block = slice(j * rows, (j + 1) * rows)
        raw = p[j][depth : depth + rows, :]
        keys = jnp.maximum(raw, 0)
        vals = p[j][depth + rows :, :HEAD_DIM]
        d_val = val_part[block, :] + dot(keys, high) + dot(keys, low)
        d_key = key_part[block, :] + dot(vals, high, ((1,), (1,))) + dot(vals, low, ((1,), (1,)))
        out[:, :HEAD_DIM] = att[j]
        out[:, HEAD_DIM : 2 * HEAD_DIM] = d_val.astype(BF16)
        out[:, 2 * HEAD_DIM :] = jnp.where(raw.astype(F32) > 0, d_key, 0.0).astype(BF16)


def place_kernel(place, *refs):
    att, key_grad, val_grad = refs[-3:]
    q, _, _ = seat(place)
    for k, ref in enumerate(refs[:-3]):
        head = q ^ k
        att[:, lanes(head, HEAD_DIM)] = ref[:, :HEAD_DIM]
        val_grad[:, lanes(head, HEAD_DIM)] = ref[:, HEAD_DIM : 2 * HEAD_DIM]
        key_grad[:, lanes(head, FEAT)] = ref[:, 2 * HEAD_DIM :]


def body(hidden, w_query, key_input, values, cotangent):
    count = lax.axis_size("ctx")
    me = lax.axis_index("ctx")
    inner = CORES * HEADS_GROUP
    outer = count // inner
    rows, depth = key_input.shape[0], w_query.shape[0]
    if lax.axis_size("heads") > 1:
        hidden = lax.all_gather(hidden, "heads", axis=1, tiled=True)
    width = hidden.shape[1]
    place = me.astype(jnp.int32).reshape(1)

    def swap(block, bits):
        return lax.ppermute(block, "ctx", [(i, i ^ bits) for i in range(count)])

    def core_swap(block):
        return swap(block, 1)

    def chip_swap(block, k):
        return swap(block, CORES * k)

    def plane_swap(block, k):
        return swap(block, inner * k)

    def down(block, k):
        return lax.ppermute(block, "ctx", [(i, i - inner * k) for i in range(inner * k, count)])

    packs = call(
        pack_kernel,
        [((depth + 2 * rows, FEAT), BF16)] * 4,
        [place, w_query, key_input, values, cotangent],
        scratch=[pltpu.SemaphoreType.DMA((16,))],
        space=pltpu.HBM,
        mib=62,
    )
    hidden, packs = lax.optimization_barrier((hidden, packs))
    p = [packs[0]] + [chip_swap(packs[k], k) for k in (1, 2, 3)]
    h1, h2 = chip_swap(hidden, 1), chip_swap(hidden, 2)
    pay, states = call(
        functools.partial(state_kernel, rows, depth),
        [((4 * depth + HALF, FEAT), BF16), ((4, FEAT, HEAD_DIM), BF16)],
        [place, *p],
        urgent=True,
    )
    pays = [pay] + [None] * (outer - 1)
    for k in reversed(range(1, outer)):
        pays[k] = plane_swap(pay, k)
    h1, h2, pays[-1], late_pay, late_states = lax.optimization_barrier((h1, h2, pays[-1], pay, states))
    h3 = [chip_swap(h1[: rows // 2], 2), chip_swap(h2[rows // 2 :], 1)]
    h = [hidden, h1, h2, *h3]
    other_pays = [core_swap(late_pay)] + [core_swap(pays[k]) for k in range(1, outer)]
    other_states = core_swap(late_states)
    positions = 4 * rows
    att, dq_t, grown, *kept = call(
        functools.partial(attend_kernel, rows, depth, outer),
        [
            ((4, rows, HEAD_DIM), BF16),
            ((FEAT, positions), BF16),
            ((4, FEAT, HEAD_DIM), BF16),
            ((4, rows, FEAT), BF16),
            ((4, rows, HEAD_DIM), BF16),
            ((4, rows, rows), BF16),
            ((4, rows, rows), BF16),
        ],
        [place, *h, *p, *pays, *other_pays, states, other_states],
        flops=2 * positions * width * FEAT + 24 * positions * FEAT * HEAD_DIM,
        scratch=[pltpu.VMEM((width, FEAT), BF16), pltpu.VMEM((positions, FEAT), F32)],
    )
    other_grown = core_swap(grown)
    (half,) = call(
        half_kernel,
        [((HALF, HEAD_DIM), BF16)],
        [place, grown, other_grown],
        scratch=[pltpu.VMEM((FEAT, HEAD_DIM), F32)],
    )
    later = [down(half, k) for k in range(1, outer)]
    sums = [None] * outer
    for k in reversed(range(outer)):
        keep, give = call(
            functools.partial(grad_kernel, depth, k),
            [((FEAT, 4 * depth), F32), ((FEAT, 4 * depth), BF16)],
            [place, *h, dq_t],
            flops=2 * positions * width * FEAT // outer,
        )
        sums[k] = keep + core_swap(give).astype(F32)
    own = sums[0]
    arrived = [plane_swap(sums[k].astype(BF16), k) for k in reversed(range(1, outer))]
    val_part, key_part = call(
        functools.partial(side_kernel, rows),
        [((positions, HEAD_DIM), F32), ((positions, FEAT), F32)],
        [place, *kept],
        flops=6 * positions * FEAT * HEAD_DIM,
    )
    rest = sum((x.astype(F32) for x in later), jnp.zeros((HALF, HEAD_DIM), F32)).astype(BF16)
    other_rest = core_swap(rest)
    outs = call(
        functools.partial(finish_kernel, rows, depth, outer),
        [((rows, 2 * HEAD_DIM + FEAT), BF16)] * 4,
        [place, *p, att, val_part, key_part, grown, other_grown, rest, other_rest],
        flops=16 * positions * FEAT * HEAD_DIM,
        scratch=[pltpu.VMEM((FEAT, HEAD_DIM), F32)],
    )
    placed = [outs[0]] + [chip_swap(outs[k], k) for k in (1, 2, 3)]
    attended, key_grad, value_grad = call(
        place_kernel,
        [
            ((rows, HEADS_GROUP * HEAD_DIM), BF16),
            ((rows, HEADS_GROUP * FEAT), BF16),
            ((rows, HEADS_GROUP * HEAD_DIM), BF16),
        ],
        [place, *placed],
    )
    blocks = call(
        functools.partial(sum_kernel, depth),
        [((FEAT, depth), F32)] + [((FEAT, depth), BF16)] * 3,
        [place, own, *arrived],
        scratch=[pltpu.VMEM((4, FEAT, depth), F32)],
        urgent=True,
    )
    columns = [blocks[0]] + [chip_swap(blocks[k], k) for k in (1, 2, 3)]
    (query_grad,) = call(
        query_grad_kernel, [((depth, HEADS_GROUP * FEAT), F32)], [place, *columns]
    )
    return (attended, query_grad, key_grad, value_grad)


def solution(mesh):
    return jax.shard_map(
        body,
        mesh=mesh,
        in_specs=(P("ctx", "heads"),) * 5,
        out_specs=(P("ctx", "heads"),) * 4,
        check_vma=False,
    )
```

```python
import functools

import jax
import jax.numpy as jnp
from jax import lax
from jax.experimental import pallas as pl
from jax.experimental.pallas import tpu as pltpu
from jax.sharding import PartitionSpec as P

HEAD_DIM = 128
FEAT = 256
HEADS_GROUP = 4
CORES = 2
EPSILON = 1e-06

F32 = jnp.float32
BF16 = jnp.bfloat16
HALF = FEAT // 2
URGENT = 1 << 35


def dot(a, b, dims=((1,), (0,))):
    return lax.dot_general(a, b, (dims, ((), ())), preferred_element_type=F32)


def split(x):
    high = x.astype(BF16)
    return high, (x - high.astype(F32)).astype(BF16)


def seat(place):
    me = place[0]
    low, high = CORES.bit_length() - 1, (CORES * HEADS_GROUP).bit_length() - 1
    return me >> low & HEADS_GROUP - 1, me >> high, me & CORES - 1


def call(kernel, outs, args, flops=0, scratch=(), mib=16, space=pltpu.VMEM, urgent=0):
    shapes = [jax.ShapeDtypeStruct(shape, dtype) for shape, dtype in outs]
    moved = sum(a.size * a.dtype.itemsize for a in args) + sum(s.size * s.dtype.itemsize for s in shapes)
    return pl.pallas_call(
        kernel,
        out_shape=shapes,
        in_specs=[pl.BlockSpec(memory_space=pltpu.SMEM)]
        + [pl.BlockSpec(memory_space=space)] * (len(args) - 1),
        out_specs=[pl.BlockSpec(memory_space=pltpu.VMEM)] * len(shapes),
        scratch_shapes=list(scratch),
        compiler_params=pltpu.CompilerParams(vmem_limit_bytes=mib << 20),
        cost_estimate=pl.CostEstimate(flops=urgent or flops, bytes_accessed=moved, transcendentals=0),
    )(*args)


def lanes(index, width):
    return pl.ds(pl.multiple_of(index * width, width), width)


def pack_kernel(place, w, key, val, cot, *refs):
    outs, sems = refs[:4], refs[4]
    rows, depth = key.shape[0], w.shape[0]
    q, _, _ = seat(place)
    copies = []
    for k in (3, 1, 2, 0):
        head, out = q ^ k, outs[k]
        low, high = pl.ds(depth, rows), pl.ds(depth + rows, rows)
        moves = (
            (w.at[:, lanes(head, FEAT)], out.at[pl.ds(0, depth), :]),
            (key.at[:, lanes(head, FEAT)], out.at[low, :]),
            (val.at[:, lanes(head, HEAD_DIM)], out.at[high, pl.ds(0, HEAD_DIM)]),
            (cot.at[:, lanes(head, HEAD_DIM)], out.at[high, pl.ds(HEAD_DIM, HEAD_DIM)]),
        )
        for source, target in moves:
            copies.append(pltpu.make_async_copy(source, target, sems.at[len(copies)]))
            copies[-1].start()
    for copy in copies:
        copy.wait()


def state_of(p, rows, depth):
    keys = jnp.maximum(p[depth : depth + rows, :], 0)
    return dot(keys, p[depth + rows :, :HEAD_DIM], ((0,), (0,)))


def own_kernel(rows, depth, place, p, shard, state):
    shard[...] = p[:depth, :]
    state[...] = state_of(p, rows, depth)


def state_kernel(rows, depth, place, shard, own_state, p1, p2, p3, pay, states):
    pay[:depth, :] = shard[...]
    total = own_state[...]
    states[0] = total.astype(BF16)
    for j, p in ((1, p1), (2, p2), (3, p3)):
        pay[j * depth : (j + 1) * depth, :] = p[:depth, :]
        state = state_of(p, rows, depth)
        states[j] = state.astype(BF16)
        total = total + state
    total = total.astype(BF16)
    pay[4 * depth :, :HEAD_DIM] = total[:HALF, :]
    pay[4 * depth :, HEAD_DIM:] = total[HALF:, :]


def hidden_columns(h, start, width):
    cols = pl.ds(start, width)
    return jnp.concatenate([ref[:, cols] for ref in h], axis=0)


def before(there, here):
    return (there < here).astype(jnp.int32).astype(F32)


def attend_kernel(rows, depth, outer, place, *refs):
    h, refs = refs[:5], refs[5:]
    p, refs = refs[:4], refs[4:]
    own_pay, refs = refs[:outer], refs[outer:]
    other_pay, refs = refs[:outer], refs[outer:]
    own_states, other_states, att, dq_t, grown, feats_out, d_num_out, scores_out, mixed_out, weights, proj = refs
    q, z, core = seat(place)
    base = jnp.zeros((FEAT, HEAD_DIM), F32)
    for k in range(outer):
        for flip, pay in ((0, own_pay[k]), (1, other_pay[k])):
            for j in range(4):
                at = (((z ^ k) * 4 + (q ^ j)) * CORES + (core ^ flip)) * depth
                weights[pl.ds(pl.multiple_of(at, depth), depth), :] = pay[j * depth : (j + 1) * depth, :]
            if k:
                packed = pay[4 * depth :, :].astype(F32)
                base = base + before(z ^ k, z) * jnp.concatenate(
                    [packed[:, :HEAD_DIM], packed[:, HEAD_DIM:]], axis=0
                )
    width = h[0].shape[1]
    step = min(512, width)
    for at in range(0, width, step):
        part = dot(hidden_columns(h, at, step), weights[at : at + step, :])
        if at:
            proj[...] += part
        else:
            proj[...] = part
    own = [own_states[j].astype(F32) for j in range(4)]
    other = [other_states[j].astype(F32) for j in range(4)]
    causal = lax.broadcasted_iota(jnp.int32, (rows, rows), 0) >= lax.broadcasted_iota(
        jnp.int32, (rows, rows), 1
    )
    for j in range(4):
        here = (q ^ j) * CORES + core
        prior = base
        for i in range(4):
            for flip, group in ((0, own), (1, other)):
                if flip == 0 and i == j:
                    continue
                prior = prior + before((q ^ i) * CORES + (core ^ flip), here) * group[i]
        prior_high, prior_low = split(prior)
        block = slice(j * rows, (j + 1) * rows)
        query = proj[block, :]
        feats = jnp.maximum(query, 0.0).astype(BF16)
        keys = jnp.maximum(p[j][depth : depth + rows, :], 0)
        vals = p[j][depth + rows :, :HEAD_DIM]
        grad = p[j][depth + rows :, HEAD_DIM:].astype(F32)
        scores = jnp.where(causal, dot(feats, keys, ((1,), (1,))), 0.0).astype(BF16)
        numer = dot(scores, vals) + dot(feats, prior_high) + dot(feats, prior_low)
        inv = lax.rsqrt(jnp.mean(numer * numer, axis=-1, keepdims=True) + EPSILON)
        normed = numer * inv
        att[j] = normed.astype(BF16)
        d_num = (inv * (grad - normed * jnp.mean(grad * normed, axis=-1, keepdims=True))).astype(BF16)
        mixed = jnp.where(causal, dot(d_num, vals, ((1,), (1,))), 0.0).astype(BF16)
        d_feat = dot(mixed, keys) + dot(d_num, prior_high, ((1,), (1,))) + dot(d_num, prior_low, ((1,), (1,)))
        d_query = jnp.where(query > 0, d_feat, 0.0)
        dq_t[:, block] = d_query.T.astype(BF16)
        grown[j] = dot(feats, d_num, ((0,), (0,))).astype(BF16)
        feats_out[j] = feats
        d_num_out[j] = d_num
        scores_out[j] = scores
        mixed_out[j] = mixed


def half_kernel(place, own, other, half, total):
    _, _, core = seat(place)
    total[...] = sum(ref[j].astype(F32) for ref in (own, other) for j in range(4))
    half[...] = total[pl.ds(pl.multiple_of(core * HALF, HALF), HALF), :].astype(BF16)


def side_kernel(rows, place, feats, d_num, scores, mixed, val_part, key_part):
    for j in range(4):
        block = slice(j * rows, (j + 1) * rows)
        val_part[block, :] = dot(scores[j], d_num[j], ((0,), (0,)))
        key_part[block, :] = dot(mixed[j], feats[j], ((0,), (0,)))


def grad_kernel(depth, k, place, *refs):
    *h, dq_t, keep, give = refs
    _, z, core = seat(place)
    pair = CORES * depth
    lhs = dq_t[...]
    for i in range(4):
        start = pl.multiple_of(((z ^ k) * 4 + i) * pair, pair)
        out = dot(lhs, hidden_columns(h, start, pair))
        even, odd = out[:, :depth], out[:, depth:]
        first = jnp.broadcast_to(core == 0, even.shape)
        keep[:, i * depth : (i + 1) * depth] = jnp.where(first, even, odd)
        give[:, i * depth : (i + 1) * depth] = jnp.where(first, odd, even).astype(BF16)


def sum_kernel(depth, place, own, *refs):
    arrived, (mine, *outs), blocks = refs[:-5], refs[-5:-1], refs[-1]
    total = own[...]
    for ref in arrived:
        total = total + ref[...].astype(F32)
    q, _, _ = seat(place)
    for i in range(4):
        blocks[q ^ i] = total[:, i * depth : (i + 1) * depth]
    mine[...] = blocks[0]
    for k, out in enumerate(outs):
        out[...] = blocks[k + 1].astype(BF16)


def query_grad_kernel(place, *refs):
    out = refs[-1]
    q, _, _ = seat(place)
    for k, ref in enumerate(refs[:-1]):
        out[:, lanes(q ^ k, FEAT)] = ref[...].astype(F32).T


def finish_kernel(rows, depth, outer, place, *refs):
    p, refs = refs[:4], refs[4:]
    att, val_part, key_part, own_grown, other_grown, own_rest, other_rest, *outs, rest = refs
    q, _, core = seat(place)
    for flip, ref in ((0, own_rest), (1, other_rest)):
        rest[pl.ds(pl.multiple_of((core ^ flip) * HALF, HALF), HALF), :] = ref[...].astype(F32)
    base = rest[...]
    own = [own_grown[j].astype(F32) for j in range(4)]
    other = [other_grown[j].astype(F32) for j in range(4)]
    for j, out in enumerate(outs):
        here = (q ^ j) * CORES + core
        later = base
        for i in range(4):
            for flip, group in ((0, own), (1, other)):
                if flip == 0 and i == j:
                    continue
                later = later + before(here, (q ^ i) * CORES + (core ^ flip)) * group[i]
        high, low = split(later)
        block = slice(j * rows, (j + 1) * rows)
        raw = p[j][depth : depth + rows, :]
        keys = jnp.maximum(raw, 0)
        vals = p[j][depth + rows :, :HEAD_DIM]
        d_val = val_part[block, :] + dot(keys, high) + dot(keys, low)
        d_key = key_part[block, :] + dot(vals, high, ((1,), (1,))) + dot(vals, low, ((1,), (1,)))
        out[:, :HEAD_DIM] = att[j]
        out[:, HEAD_DIM : 2 * HEAD_DIM] = d_val.astype(BF16)
        out[:, 2 * HEAD_DIM :] = jnp.where(raw.astype(F32) > 0, d_key, 0.0).astype(BF16)


def place_kernel(place, *refs):
    att, key_grad, val_grad = refs[-3:]
    q, _, _ = seat(place)
    for k, ref in enumerate(refs[:-3]):
        head = q ^ k
        att[:, lanes(head, HEAD_DIM)] = ref[:, :HEAD_DIM]
        val_grad[:, lanes(head, HEAD_DIM)] = ref[:, HEAD_DIM : 2 * HEAD_DIM]
        key_grad[:, lanes(head, FEAT)] = ref[:, 2 * HEAD_DIM :]


def body(hidden, w_query, key_input, values, cotangent):
    count = lax.axis_size("ctx")
    me = lax.axis_index("ctx")
    inner = CORES * HEADS_GROUP
    outer = count // inner
    rows, depth = key_input.shape[0], w_query.shape[0]
    if lax.axis_size("heads") > 1:
        hidden = lax.all_gather(hidden, "heads", axis=1, tiled=True)
    width = hidden.shape[1]
    place = me.astype(jnp.int32).reshape(1)

    def swap(block, bits):
        return lax.ppermute(block, "ctx", [(i, i ^ bits) for i in range(count)])

    def core_swap(block):
        return swap(block, 1)

    def chip_swap(block, k):
        return swap(block, CORES * k)

    def plane_swap(block, k):
        return swap(block, inner * k)

    def down(block, k):
        return lax.ppermute(block, "ctx", [(i, i - inner * k) for i in range(inner * k, count)])

    packs = call(
        pack_kernel,
        [((depth + 2 * rows, FEAT), BF16)] * 4,
        [place, w_query, key_input, values, cotangent],
        scratch=[pltpu.SemaphoreType.DMA((16,))],
        space=pltpu.HBM,
        mib=59,
    )
    hidden, packs = lax.optimization_barrier((hidden, packs))
    p = [packs[0]] + [chip_swap(packs[k], k) for k in (1, 2, 3)]
    h1, h2 = chip_swap(hidden, 1), chip_swap(hidden, 2)
    start = call(
        functools.partial(own_kernel, rows, depth),
        [((depth, FEAT), BF16), ((FEAT, HEAD_DIM), F32)],
        [place, p[0]],
    )
    pay, states = call(
        functools.partial(state_kernel, rows, depth),
        [((4 * depth + HALF, FEAT), BF16), ((4, FEAT, HEAD_DIM), BF16)],
        [place, *start, *p[1:]],
        urgent=URGENT,
    )
    pays = [pay] + [None] * (outer - 1)
    for k in sorted(range(1, outer), key=lambda k: (k.bit_count(), -k)):
        pays[k] = plane_swap(pays[k & k - 1], k & -k)
    h1, h2, late_pay, late_states = lax.optimization_barrier((h1, h2, pay, states))
    h3 = [chip_swap(h1[: rows // 2], 2), chip_swap(h2[rows // 2 :], 1)]
    h = [hidden, h1, h2, *h3]
    other_pays = [core_swap(late_pay)] + [core_swap(pays[k]) for k in range(1, outer)]
    other_states = core_swap(late_states)
    positions = 4 * rows
    att, dq_t, grown, *kept = call(
        functools.partial(attend_kernel, rows, depth, outer),
        [
            ((4, rows, HEAD_DIM), BF16),
            ((FEAT, positions), BF16),
            ((4, FEAT, HEAD_DIM), BF16),
            ((4, rows, FEAT), BF16),
            ((4, rows, HEAD_DIM), BF16),
            ((4, rows, rows), BF16),
            ((4, rows, rows), BF16),
        ],
        [place, *h, *p, *pays, *other_pays, states, other_states],
        flops=2 * positions * width * FEAT + 24 * positions * FEAT * HEAD_DIM,
        scratch=[pltpu.VMEM((width, FEAT), BF16), pltpu.VMEM((positions, FEAT), F32)],
    )
    other_grown = core_swap(grown)
    (half,) = call(
        half_kernel,
        [((HALF, HEAD_DIM), BF16)],
        [place, grown, other_grown],
        scratch=[pltpu.VMEM((FEAT, HEAD_DIM), F32)],
    )
    rest, window, step = jnp.zeros(half.shape, F32), half, 1
    while step < outer:
        came = down(window, step)
        rest = rest + came.astype(F32)
        window = (window.astype(F32) + came.astype(F32)).astype(BF16)
        step *= 2
    sums = [None] * outer
    order = sorted(range(outer), key=lambda k: (-k.bit_count(), k))
    for k in order:
        keep, give = call(
            functools.partial(grad_kernel, depth, k),
            [((FEAT, 4 * depth), F32), ((FEAT, 4 * depth), BF16)],
            [place, *h, dq_t],
            flops=2 * positions * width * FEAT // outer,
        )
        sums[k] = keep + core_swap(give).astype(F32)
    arrived = []
    for k in order[:-1]:
        came, onward = plane_swap(sums[k].astype(BF16), k & -k), k & k - 1
        if onward:
            sums[onward] = sums[onward] + came.astype(F32)
        else:
            arrived.append(came)
    own = sums[0]
    val_part, key_part = call(
        functools.partial(side_kernel, rows),
        [((positions, HEAD_DIM), F32), ((positions, FEAT), F32)],
        [place, *kept],
        flops=6 * positions * FEAT * HEAD_DIM,
    )
    rest = rest.astype(BF16)
    other_rest = core_swap(rest)
    outs = call(
        functools.partial(finish_kernel, rows, depth, outer),
        [((rows, 2 * HEAD_DIM + FEAT), BF16)] * 4,
        [place, *p, att, val_part, key_part, grown, other_grown, rest, other_rest],
        flops=16 * positions * FEAT * HEAD_DIM,
        scratch=[pltpu.VMEM((FEAT, HEAD_DIM), F32)],
    )
    placed = [outs[0]] + [chip_swap(outs[k], k) for k in (1, 2, 3)]
    attended, key_grad, value_grad = call(
        place_kernel,
        [
            ((rows, HEADS_GROUP * HEAD_DIM), BF16),
            ((rows, HEADS_GROUP * FEAT), BF16),
            ((rows, HEADS_GROUP * HEAD_DIM), BF16),
        ],
        [place, *placed],
    )
    own, placed = lax.optimization_barrier((own, placed))
    blocks = call(
        functools.partial(sum_kernel, depth),
        [((FEAT, depth), F32)] + [((FEAT, depth), BF16)] * 3,
        [place, own, *arrived],
        scratch=[pltpu.VMEM((4, FEAT, depth), F32)],
        urgent=URGENT,
    )
    columns = [blocks[0]] + [chip_swap(blocks[k], k) for k in (1, 2, 3)]
    (query_grad,) = call(
        query_grad_kernel, [((depth, HEADS_GROUP * FEAT), F32)], [place, *columns]
    )
    return (attended, query_grad, key_grad, value_grad)


def solution(mesh):
    return jax.shard_map(
        body,
        mesh=mesh,
        in_specs=(P("ctx", "heads"),) * 5,
        out_specs=(P("ctx", "heads"),) * 4,
        check_vma=False,
    )
```

```python
import functools

import jax
import jax.numpy as jnp
from jax import lax
from jax.experimental import pallas as pl
from jax.experimental.pallas import tpu as pltpu
from jax.sharding import PartitionSpec as P

HEAD_DIM = 128
FEAT = 256
HEADS_GROUP = 4
CORES = 2
EPSILON = 1e-06

F32 = jnp.float32
BF16 = jnp.bfloat16
HALF = FEAT // 2
URGENT = 1 << 35


def dot(a, b, dims=((1,), (0,))):
    return lax.dot_general(a, b, (dims, ((), ())), preferred_element_type=F32)


def split(x):
    high = x.astype(BF16)
    return high, (x - high.astype(F32)).astype(BF16)


def seat(place):
    me = place[0]
    low, high = CORES.bit_length() - 1, (CORES * HEADS_GROUP).bit_length() - 1
    return me >> low & HEADS_GROUP - 1, me >> high, me & CORES - 1


def call(kernel, outs, args, flops=0, scratch=(), mib=16, space=pltpu.VMEM, urgent=0):
    shapes = [jax.ShapeDtypeStruct(shape, dtype) for shape, dtype in outs]
    moved = sum(a.size * a.dtype.itemsize for a in args) + sum(s.size * s.dtype.itemsize for s in shapes)
    return pl.pallas_call(
        kernel,
        out_shape=shapes,
        in_specs=[pl.BlockSpec(memory_space=pltpu.SMEM)]
        + [pl.BlockSpec(memory_space=space)] * (len(args) - 1),
        out_specs=[pl.BlockSpec(memory_space=pltpu.VMEM)] * len(shapes),
        scratch_shapes=list(scratch),
        compiler_params=pltpu.CompilerParams(vmem_limit_bytes=mib << 20),
        cost_estimate=pl.CostEstimate(flops=urgent or flops, bytes_accessed=moved, transcendentals=0),
    )(*args)


def lanes(index, width):
    return pl.ds(pl.multiple_of(index * width, width), width)


def pack_kernel(place, w, key, val, cot, *refs):
    outs, sems = refs[:4], refs[4]
    rows, depth = key.shape[0], w.shape[0]
    q, _, _ = seat(place)
    copies = []
    for k in (3, 1, 2, 0):
        head, out = q ^ k, outs[k]
        low, high = pl.ds(depth, rows), pl.ds(depth + rows, rows)
        moves = (
            (w.at[:, lanes(head, FEAT)], out.at[pl.ds(0, depth), :]),
            (key.at[:, lanes(head, FEAT)], out.at[low, :]),
            (val.at[:, lanes(head, HEAD_DIM)], out.at[high, pl.ds(0, HEAD_DIM)]),
            (cot.at[:, lanes(head, HEAD_DIM)], out.at[high, pl.ds(HEAD_DIM, HEAD_DIM)]),
        )
        for source, target in moves:
            copies.append(pltpu.make_async_copy(source, target, sems.at[len(copies)]))
            copies[-1].start()
    for copy in copies:
        copy.wait()


def state_of(p, rows, depth):
    keys = jnp.maximum(p[depth : depth + rows, :], 0)
    return dot(keys, p[depth + rows :, :HEAD_DIM], ((0,), (0,)))


def own_kernel(rows, depth, place, p, shard, state):
    shard[...] = p[:depth, :]
    state[...] = state_of(p, rows, depth)


def state_kernel(rows, depth, place, shard, own_state, p1, p2, p3, pay, states):
    pay[:depth, :] = shard[...]
    total = own_state[...]
    states[0] = total.astype(BF16)
    for j, p in ((1, p1), (2, p2), (3, p3)):
        pay[j * depth : (j + 1) * depth, :] = p[:depth, :]
        state = state_of(p, rows, depth)
        states[j] = state.astype(BF16)
        total = total + state
    total = total.astype(BF16)
    pay[4 * depth :, :HEAD_DIM] = total[:HALF, :]
    pay[4 * depth :, HEAD_DIM:] = total[HALF:, :]


def hidden_columns(h, start, width):
    cols = pl.ds(start, width)
    return jnp.concatenate([ref[:, cols] for ref in h], axis=0)


def before(there, here):
    return (there < here).astype(jnp.int32).astype(F32)


def causal_mask(rows):
    return lax.broadcasted_iota(jnp.int32, (rows, rows), 0) >= lax.broadcasted_iota(
        jnp.int32, (rows, rows), 1
    )


def attend_block(j, rows, depth, query, p, prior_high, prior_low, outs):
    att, dq_t, grown, feats_out, d_num_out, scores_out, mixed_out = outs
    causal = causal_mask(rows)
    feats = jnp.maximum(query, 0.0).astype(BF16)
    keys = jnp.maximum(p[depth : depth + rows, :], 0)
    vals = p[depth + rows :, :HEAD_DIM]
    grad = p[depth + rows :, HEAD_DIM:].astype(F32)
    scores = jnp.where(causal, dot(feats, keys, ((1,), (1,))), 0.0).astype(BF16)
    numer = dot(scores, vals) + dot(feats, prior_high) + dot(feats, prior_low)
    inv = lax.rsqrt(jnp.mean(numer * numer, axis=-1, keepdims=True) + EPSILON)
    normed = numer * inv
    att[j] = normed.astype(BF16)
    d_num = (inv * (grad - normed * jnp.mean(grad * normed, axis=-1, keepdims=True))).astype(BF16)
    mixed = jnp.where(causal, dot(d_num, vals, ((1,), (1,))), 0.0).astype(BF16)
    d_feat = dot(mixed, keys) + dot(d_num, prior_high, ((1,), (1,))) + dot(d_num, prior_low, ((1,), (1,)))
    d_query = jnp.where(query > 0, d_feat, 0.0)
    dq_t[:, j * rows : (j + 1) * rows] = d_query.T.astype(BF16)
    grown[j] = dot(feats, d_num, ((0,), (0,))).astype(BF16)
    feats_out[j] = feats
    d_num_out[j] = d_num
    scores_out[j] = scores
    mixed_out[j] = mixed


def attend_kernel(rows, depth, outer, place, *refs):
    h, refs = refs[:3], refs[3:]
    p, refs = refs[:3], refs[3:]
    own_pay, refs = refs[:outer], refs[outer:]
    other_pay, refs = refs[:outer], refs[outer:]
    own_states, other_states, *outs, weights, last_high, last_low, proj = refs
    q, z, core = seat(place)
    base = jnp.zeros((FEAT, HEAD_DIM), F32)
    for k in range(outer):
        for flip, pay in ((0, own_pay[k]), (1, other_pay[k])):
            for j in range(4):
                at = (((z ^ k) * 4 + (q ^ j)) * CORES + (core ^ flip)) * depth
                weights[pl.ds(pl.multiple_of(at, depth), depth), :] = pay[j * depth : (j + 1) * depth, :]
            if k:
                packed = pay[4 * depth :, :].astype(F32)
                base = base + before(z ^ k, z) * jnp.concatenate(
                    [packed[:, :HEAD_DIM], packed[:, HEAD_DIM:]], axis=0
                )
    width = h[0].shape[1]
    step = min(512, width)
    for at in range(0, width, step):
        part = dot(hidden_columns(h, at, step), weights[at : at + step, :])
        if at:
            proj[...] += part
        else:
            proj[...] = part
    own = [own_states[j].astype(F32) for j in range(4)]
    other = [other_states[j].astype(F32) for j in range(4)]
    for j in range(4):
        here = (q ^ j) * CORES + core
        prior = base
        for i in range(4):
            for flip, group in ((0, own), (1, other)):
                if flip == 0 and i == j:
                    continue
                prior = prior + before((q ^ i) * CORES + (core ^ flip), here) * group[i]
        high, low = split(prior)
        if j < 3:
            attend_block(j, rows, depth, proj[j * rows : (j + 1) * rows, :], p[j], high, low, outs)
        else:
            last_high[...] = high
            last_low[...] = low


def last_kernel(rows, depth, place, top, bottom, weights, p, high, low, *outs):
    query = dot(jnp.concatenate([top[...], bottom[...]], axis=0), weights[...])
    attend_block(0, rows, depth, query, p, high[...], low[...], outs)


def half_kernel(place, *refs):
    *parts, half, total = refs
    _, _, core = seat(place)
    total[...] = sum(ref[j].astype(F32) for ref in parts for j in range(ref.shape[0]))
    half[...] = total[pl.ds(pl.multiple_of(core * HALF, HALF), HALF), :].astype(BF16)


def side_kernel(place, feats, d_num, scores, mixed, val_part, key_part):
    for j in range(feats.shape[0]):
        val_part[j] = dot(scores[j], d_num[j], ((0,), (0,)))
        key_part[j] = dot(mixed[j], feats[j], ((0,), (0,)))


def grad_kernel(depth, k, place, *refs):
    *h, dq_first, dq_last, keep, give = refs
    _, z, core = seat(place)
    pair = CORES * depth
    lhs = jnp.concatenate([dq_first[...], dq_last[...]], axis=1)
    for i in range(4):
        start = pl.multiple_of(((z ^ k) * 4 + i) * pair, pair)
        out = dot(lhs, hidden_columns(h, start, pair))
        even, odd = out[:, :depth], out[:, depth:]
        first = jnp.broadcast_to(core == 0, even.shape)
        keep[:, i * depth : (i + 1) * depth] = jnp.where(first, even, odd)
        give[:, i * depth : (i + 1) * depth] = jnp.where(first, odd, even).astype(BF16)


def sum_kernel(depth, place, own, *refs):
    arrived, (mine, *outs), blocks = refs[:-5], refs[-5:-1], refs[-1]
    total = own[...]
    for ref in arrived:
        total = total + ref[...].astype(F32)
    q, _, _ = seat(place)
    for i in range(4):
        blocks[q ^ i] = total[:, i * depth : (i + 1) * depth]
    mine[...] = blocks[0]
    for k, out in enumerate(outs):
        out[...] = blocks[k + 1].astype(BF16)


def query_grad_kernel(place, *refs):
    out = refs[-1]
    q, _, _ = seat(place)
    for k, ref in enumerate(refs[:-1]):
        out[:, lanes(q ^ k, FEAT)] = ref[...].astype(F32).T


def finish_kernel(rows, depth, outer, place, *refs):
    p, refs = refs[:4], refs[4:]
    pairs, (own_rest, other_rest, *outs, rest) = refs[:10], refs[10:]
    att, val_part, key_part, own_grown, other_grown = (
        [*(first.at[j] for j in range(3)), last.at[0]] for first, last in zip(pairs[:5], pairs[5:])
    )
    q, _, core = seat(place)
    for flip, ref in ((0, own_rest), (1, other_rest)):
        rest[pl.ds(pl.multiple_of((core ^ flip) * HALF, HALF), HALF), :] = ref[...].astype(F32)
    base = rest[...]
    own = [ref[...].astype(F32) for ref in own_grown]
    other = [ref[...].astype(F32) for ref in other_grown]
    for j, out in enumerate(outs):
        here = (q ^ j) * CORES + core
        later = base
        for i in range(4):
            for flip, group in ((0, own), (1, other)):
                if flip == 0 and i == j:
                    continue
                later = later + before(here, (q ^ i) * CORES + (core ^ flip)) * group[i]
        high, low = split(later)
        raw = p[j][depth : depth + rows, :]
        keys = jnp.maximum(raw, 0)
        vals = p[j][depth + rows :, :HEAD_DIM]
        d_val = val_part[j][...] + dot(keys, high) + dot(keys, low)
        d_key = key_part[j][...] + dot(vals, high, ((1,), (1,))) + dot(vals, low, ((1,), (1,)))
        out[:, :HEAD_DIM] = att[j][...]
        out[:, HEAD_DIM : 2 * HEAD_DIM] = d_val.astype(BF16)
        out[:, 2 * HEAD_DIM :] = jnp.where(raw.astype(F32) > 0, d_key, 0.0).astype(BF16)


def place_kernel(place, *refs):
    att, key_grad, val_grad = refs[-3:]
    q, _, _ = seat(place)
    for k, ref in enumerate(refs[:-3]):
        head = q ^ k
        att[:, lanes(head, HEAD_DIM)] = ref[:, :HEAD_DIM]
        val_grad[:, lanes(head, HEAD_DIM)] = ref[:, HEAD_DIM : 2 * HEAD_DIM]
        key_grad[:, lanes(head, FEAT)] = ref[:, 2 * HEAD_DIM :]


def body(hidden, w_query, key_input, values, cotangent):
    count = lax.axis_size("ctx")
    me = lax.axis_index("ctx")
    inner = CORES * HEADS_GROUP
    outer = count // inner
    rows, depth = key_input.shape[0], w_query.shape[0]
    if lax.axis_size("heads") > 1:
        hidden = lax.all_gather(hidden, "heads", axis=1, tiled=True)
    width = hidden.shape[1]
    place = me.astype(jnp.int32).reshape(1)

    def swap(block, bits):
        return lax.ppermute(block, "ctx", [(i, i ^ bits) for i in range(count)])

    def core_swap(block):
        return swap(block, 1)

    def chip_swap(block, k):
        return swap(block, CORES * k)

    def plane_swap(block, k):
        return swap(block, inner * k)

    def down(block, k):
        return lax.ppermute(block, "ctx", [(i, i - inner * k) for i in range(inner * k, count)])

    packs = call(
        pack_kernel,
        [((depth + 2 * rows, FEAT), BF16)] * 4,
        [place, w_query, key_input, values, cotangent],
        scratch=[pltpu.SemaphoreType.DMA((16,))],
        space=pltpu.HBM,
        mib=59,
    )
    hidden, packs = lax.optimization_barrier((hidden, packs))
    p = [packs[0]] + [chip_swap(packs[k], k) for k in (1, 2, 3)]
    h1, h2 = chip_swap(hidden, 1), chip_swap(hidden, 2)
    start = call(
        functools.partial(own_kernel, rows, depth),
        [((depth, FEAT), BF16), ((FEAT, HEAD_DIM), F32)],
        [place, p[0]],
    )
    pay, states = call(
        functools.partial(state_kernel, rows, depth),
        [((4 * depth + HALF, FEAT), BF16), ((4, FEAT, HEAD_DIM), BF16)],
        [place, *start, *p[1:]],
        urgent=URGENT,
    )
    pays = [pay] + [None] * (outer - 1)
    for k in sorted(range(1, outer), key=lambda k: (k.bit_count(), -k)):
        pays[k] = plane_swap(pays[k & k - 1], k & -k)
    h1, h2, late_pay, late_states = lax.optimization_barrier((h1, h2, pay, states))
    h3 = [chip_swap(h1[: rows // 2], 2), chip_swap(h2[rows // 2 :], 1)]
    h = [hidden, h1, h2, *h3]
    other_pays = [core_swap(late_pay)] + [core_swap(pays[k]) for k in range(1, outer)]
    other_states = core_swap(late_states)
    positions = 4 * rows

    def kept(blocks):
        return [
            ((blocks, rows, HEAD_DIM), BF16),
            ((FEAT, blocks * rows), BF16),
            ((blocks, FEAT, HEAD_DIM), BF16),
            ((blocks, rows, FEAT), BF16),
            ((blocks, rows, HEAD_DIM), BF16),
            ((blocks, rows, rows), BF16),
            ((blocks, rows, rows), BF16),
        ]

    def side(parts):
        blocks = parts[0].shape[0]
        return call(
            side_kernel,
            [((blocks, rows, HEAD_DIM), F32), ((blocks, rows, FEAT), F32)],
            [place, *parts],
            flops=6 * blocks * rows * FEAT * HEAD_DIM,
        )

    *first, weights, high, low = call(
        functools.partial(attend_kernel, rows, depth, outer),
        kept(3) + [((width, FEAT), BF16), ((FEAT, HEAD_DIM), BF16), ((FEAT, HEAD_DIM), BF16)],
        [place, hidden, h1, h2, *p[:3], *pays, *other_pays, states, other_states],
        flops=2 * 3 * rows * width * FEAT,
        scratch=[pltpu.VMEM((3 * rows, FEAT), F32)],
    )
    last = call(
        functools.partial(last_kernel, rows, depth),
        kept(1),
        [place, *h3, weights, p[3], high, low],
        flops=2 * rows * width * FEAT,
    )
    others = [core_swap(first[2]), core_swap(last[2])]
    (half,) = call(
        half_kernel,
        [((HALF, HEAD_DIM), BF16)],
        [place, first[2], last[2], *others],
        scratch=[pltpu.VMEM((FEAT, HEAD_DIM), F32)],
    )
    sums = [None] * outer
    order = sorted(range(outer), key=lambda k: (-k.bit_count(), k))
    dq_first, dq_last = first[1], last[1]
    for k in order:
        keep, give = call(
            functools.partial(grad_kernel, depth, k),
            [((FEAT, 4 * depth), F32), ((FEAT, 4 * depth), BF16)],
            [place, *h, dq_first, dq_last],
            flops=2 * positions * width * FEAT // outer,
        )
        sums[k] = keep + core_swap(give).astype(F32)
        if k == order[0]:
            sums[k], half = lax.optimization_barrier((sums[k].astype(BF16), half))
    rest, window, step = jnp.zeros(half.shape, F32), half, 1
    while step < outer:
        came = down(window, step)
        rest = rest + came.astype(F32)
        window = (window.astype(F32) + came.astype(F32)).astype(BF16)
        step *= 2
    arrived = []
    for k in order[:-1]:
        came, onward = plane_swap(sums[k].astype(BF16), k & -k), k & k - 1
        if onward:
            sums[onward] = sums[onward] + came.astype(F32)
        else:
            arrived.append(came)
    own = sums[0]
    rest = rest.astype(BF16)
    other_rest = core_swap(rest)
    outs = call(
        functools.partial(finish_kernel, rows, depth, outer),
        [((rows, 2 * HEAD_DIM + FEAT), BF16)] * 4,
        [
            place,
            *p,
            *(first[0], *side(first[3:]), first[2], others[0]),
            *(last[0], *side(last[3:]), last[2], others[1]),
            rest,
            other_rest,
        ],
        flops=16 * positions * FEAT * HEAD_DIM,
        scratch=[pltpu.VMEM((FEAT, HEAD_DIM), F32)],
    )
    placed = [outs[0]] + [chip_swap(outs[k], k) for k in (1, 2, 3)]
    attended, key_grad, value_grad = call(
        place_kernel,
        [
            ((rows, HEADS_GROUP * HEAD_DIM), BF16),
            ((rows, HEADS_GROUP * FEAT), BF16),
            ((rows, HEADS_GROUP * HEAD_DIM), BF16),
        ],
        [place, *placed],
    )
    own, placed = lax.optimization_barrier((own, placed))
    blocks = call(
        functools.partial(sum_kernel, depth),
        [((FEAT, depth), F32)] + [((FEAT, depth), BF16)] * 3,
        [place, own, *arrived],
        scratch=[pltpu.VMEM((4, FEAT, depth), F32)],
        urgent=URGENT,
    )
    columns = [blocks[0]] + [chip_swap(blocks[k], k) for k in (1, 2, 3)]
    (query_grad,) = call(
        query_grad_kernel, [((depth, HEADS_GROUP * FEAT), F32)], [place, *columns]
    )
    return (attended, query_grad, key_grad, value_grad)


def solution(mesh):
    return jax.shard_map(
        body,
        mesh=mesh,
        in_specs=(P("ctx", "heads"),) * 5,
        out_specs=(P("ctx", "heads"),) * 4,
        check_vma=False,
    )
```

```python
import functools

import jax
import jax.numpy as jnp
from jax import lax
from jax.experimental import pallas as pl
from jax.experimental.pallas import tpu as pltpu
from jax.sharding import PartitionSpec as P

HEAD_DIM = 128
FEAT = 256
HEADS_GROUP = 4
CORES = 2
EPSILON = 1e-06

F32 = jnp.float32
BF16 = jnp.bfloat16
HALF = FEAT // 2
URGENT = 1 << 35


def dot(a, b, dims=((1,), (0,))):
    return lax.dot_general(a, b, (dims, ((), ())), preferred_element_type=F32)


def split(x):
    high = x.astype(BF16)
    return high, (x - high.astype(F32)).astype(BF16)


def seat(place):
    me = place[0]
    low, high = CORES.bit_length() - 1, (CORES * HEADS_GROUP).bit_length() - 1
    return me >> low & HEADS_GROUP - 1, me >> high, me & CORES - 1


def call(kernel, outs, args, flops=0, scratch=(), mib=16, space=pltpu.VMEM, urgent=0):
    shapes = [jax.ShapeDtypeStruct(shape, dtype) for shape, dtype in outs]
    moved = sum(a.size * a.dtype.itemsize for a in args) + sum(s.size * s.dtype.itemsize for s in shapes)
    return pl.pallas_call(
        kernel,
        out_shape=shapes,
        in_specs=[pl.BlockSpec(memory_space=pltpu.SMEM)]
        + [pl.BlockSpec(memory_space=space)] * (len(args) - 1),
        out_specs=[pl.BlockSpec(memory_space=pltpu.VMEM)] * len(shapes),
        scratch_shapes=list(scratch),
        compiler_params=pltpu.CompilerParams(vmem_limit_bytes=mib << 20),
        cost_estimate=pl.CostEstimate(flops=urgent or flops, bytes_accessed=moved, transcendentals=0),
    )(*args)


def lanes(index, width):
    return pl.ds(pl.multiple_of(index * width, width), width)


def pack_kernel(place, w, key, val, cot, *refs):
    outs, sems = refs[:4], refs[4]
    rows, depth = key.shape[0], w.shape[0]
    q, _, _ = seat(place)
    copies = []
    for k in (3, 1, 2, 0):
        head, out = q ^ k, outs[k]
        low, high = pl.ds(depth, rows), pl.ds(depth + rows, rows)
        moves = (
            (w.at[:, lanes(head, FEAT)], out.at[pl.ds(0, depth), :]),
            (key.at[:, lanes(head, FEAT)], out.at[low, :]),
            (val.at[:, lanes(head, HEAD_DIM)], out.at[high, pl.ds(0, HEAD_DIM)]),
            (cot.at[:, lanes(head, HEAD_DIM)], out.at[high, pl.ds(HEAD_DIM, HEAD_DIM)]),
        )
        for source, target in moves:
            copies.append(pltpu.make_async_copy(source, target, sems.at[len(copies)]))
            copies[-1].start()
    for copy in copies:
        copy.wait()


def state_of(p, rows, depth):
    keys = jnp.maximum(p[depth : depth + rows, :], 0)
    return dot(keys, p[depth + rows :, :HEAD_DIM], ((0,), (0,)))


def own_kernel(rows, depth, place, p, shard, state):
    shard[...] = p[:depth, :]
    state[...] = state_of(p, rows, depth)


def state_kernel(rows, depth, place, shard, own_state, p1, p2, p3, pay, states):
    pay[:depth, :] = shard[...]
    total = own_state[...]
    states[0] = total.astype(BF16)
    for j, p in ((1, p1), (2, p2), (3, p3)):
        pay[j * depth : (j + 1) * depth, :] = p[:depth, :]
        state = state_of(p, rows, depth)
        states[j] = state.astype(BF16)
        total = total + state
    total = total.astype(BF16)
    pay[4 * depth :, :HEAD_DIM] = total[:HALF, :]
    pay[4 * depth :, HEAD_DIM:] = total[HALF:, :]


def hidden_columns(h, start, width):
    cols = pl.ds(start, width)
    return jnp.concatenate([ref[:, cols] for ref in h], axis=0)


def before(there, here):
    return (there < here).astype(jnp.int32).astype(F32)


def causal_mask(rows):
    return lax.broadcasted_iota(jnp.int32, (rows, rows), 0) >= lax.broadcasted_iota(
        jnp.int32, (rows, rows), 1
    )


def attend_block(j, rows, depth, query, p, prior_high, prior_low, outs):
    att, dq_t, grown, feats_out, d_num_out, scores_out, mixed_out = outs
    causal = causal_mask(rows)
    feats = jnp.maximum(query, 0.0).astype(BF16)
    keys = jnp.maximum(p[depth : depth + rows, :], 0)
    vals = p[depth + rows :, :HEAD_DIM]
    grad = p[depth + rows :, HEAD_DIM:].astype(F32)
    scores = jnp.where(causal, dot(feats, keys, ((1,), (1,))), 0.0).astype(BF16)
    numer = dot(scores, vals) + dot(feats, prior_high) + dot(feats, prior_low)
    inv = lax.rsqrt(jnp.mean(numer * numer, axis=-1, keepdims=True) + EPSILON)
    normed = numer * inv
    att[j] = normed.astype(BF16)
    d_num = (inv * (grad - normed * jnp.mean(grad * normed, axis=-1, keepdims=True))).astype(BF16)
    mixed = jnp.where(causal, dot(d_num, vals, ((1,), (1,))), 0.0).astype(BF16)
    d_feat = dot(mixed, keys) + dot(d_num, prior_high, ((1,), (1,))) + dot(d_num, prior_low, ((1,), (1,)))
    d_query = jnp.where(query > 0, d_feat, 0.0)
    dq_t[:, j * rows : (j + 1) * rows] = d_query.T.astype(BF16)
    grown[j] = dot(feats, d_num, ((0,), (0,))).astype(BF16)
    feats_out[j] = feats
    d_num_out[j] = d_num
    scores_out[j] = scores
    mixed_out[j] = mixed


def attend_kernel(rows, depth, outer, place, *refs):
    h, refs = refs[:3], refs[3:]
    p, refs = refs[:3], refs[3:]
    own_pay, refs = refs[:outer], refs[outer:]
    other_pay, refs = refs[:outer], refs[outer:]
    own_states, other_states, *outs, weights, last_high, last_low, proj = refs
    q, z, core = seat(place)
    base = jnp.zeros((FEAT, HEAD_DIM), F32)
    for k in range(outer):
        for flip, pay in ((0, own_pay[k]), (1, other_pay[k])):
            for j in range(4):
                at = (((z ^ k) * 4 + (q ^ j)) * CORES + (core ^ flip)) * depth
                weights[pl.ds(pl.multiple_of(at, depth), depth), :] = pay[j * depth : (j + 1) * depth, :]
            if k:
                packed = pay[4 * depth :, :].astype(F32)
                base = base + before(z ^ k, z) * jnp.concatenate(
                    [packed[:, :HEAD_DIM], packed[:, HEAD_DIM:]], axis=0
                )
    width = h[0].shape[1]
    step = min(512, width)
    for at in range(0, width, step):
        part = dot(hidden_columns(h, at, step), weights[at : at + step, :])
        if at:
            proj[...] += part
        else:
            proj[...] = part
    own = [own_states[j].astype(F32) for j in range(4)]
    other = [other_states[j].astype(F32) for j in range(4)]
    for j in range(4):
        here = (q ^ j) * CORES + core
        prior = base
        for i in range(4):
            for flip, group in ((0, own), (1, other)):
                if flip == 0 and i == j:
                    continue
                prior = prior + before((q ^ i) * CORES + (core ^ flip), here) * group[i]
        high, low = split(prior)
        if j < 3:
            attend_block(j, rows, depth, proj[j * rows : (j + 1) * rows, :], p[j], high, low, outs)
        else:
            last_high[...] = high
            last_low[...] = low


def last_kernel(rows, depth, place, top, bottom, weights, p, high, low, grown, *outs):
    *outs, every = outs
    query = dot(jnp.concatenate([top[...], bottom[...]], axis=0), weights[...])
    attend_block(0, rows, depth, query, p, high[...], low[...], outs)
    every[:3] = grown[...]
    every[3] = outs[2][0]


def load_kernel(depth, place, keep, gift, *refs):
    *parts, load, half, total = refs
    _, _, core = seat(place)
    load[:FEAT, :] = (keep[...] + gift[...].astype(F32)).astype(BF16)
    total[...] = sum(ref[j].astype(F32) for ref in parts for j in range(ref.shape[0]))
    mine = total[pl.ds(pl.multiple_of(core * HALF, HALF), HALF), :].astype(BF16)
    half[...] = mine
    wide = load.shape[1] // HEAD_DIM
    tall = HALF // wide
    for i in range(wide):
        load[FEAT:, i * HEAD_DIM : (i + 1) * HEAD_DIM] = mine[i * tall : (i + 1) * tall, :]


def unload_kernel(place, load, half, came, window):
    wide = load.shape[1] // HEAD_DIM
    tall = HALF // wide
    for i in range(wide):
        came[i * tall : (i + 1) * tall, :] = load[FEAT:, i * HEAD_DIM : (i + 1) * HEAD_DIM]
    window[...] = (half[...].astype(F32) + came[...].astype(F32)).astype(BF16)


def rest_kernel(place, *refs):
    *steps, rest = refs
    _, z, _ = seat(place)
    total = jnp.zeros(rest.shape, F32)
    for i, ref in enumerate(steps):
        total = total + before(z, z ^ 1 << i) * ref[...].astype(F32)
    rest[...] = total.astype(BF16)


def side_kernel(place, feats, d_num, scores, mixed, val_part, key_part):
    for j in range(feats.shape[0]):
        val_part[j] = dot(scores[j], d_num[j], ((0,), (0,)))
        key_part[j] = dot(mixed[j], feats[j], ((0,), (0,)))


def grad_kernel(depth, k, place, *refs):
    *h, dq_first, dq_last, keep, give = refs
    _, z, core = seat(place)
    pair = CORES * depth
    lhs = jnp.concatenate([dq_first[...], dq_last[...]], axis=1)
    for i in range(4):
        start = pl.multiple_of(((z ^ k) * 4 + i) * pair, pair)
        out = dot(lhs, hidden_columns(h, start, pair))
        even, odd = out[:, :depth], out[:, depth:]
        first = jnp.broadcast_to(core == 0, even.shape)
        keep[:, i * depth : (i + 1) * depth] = jnp.where(first, even, odd)
        give[:, i * depth : (i + 1) * depth] = jnp.where(first, odd, even).astype(BF16)


def sum_kernel(depth, place, own, *refs):
    arrived, (mine, *outs), blocks = refs[:-5], refs[-5:-1], refs[-1]
    total = own[...]
    for ref in arrived:
        total = total + ref[...].astype(F32)
    q, _, _ = seat(place)
    for i in range(4):
        blocks[q ^ i] = total[:, i * depth : (i + 1) * depth]
    mine[...] = blocks[0]
    for k, out in enumerate(outs):
        out[...] = blocks[k + 1].astype(BF16)


def query_grad_kernel(place, *refs):
    out = refs[-1]
    q, _, _ = seat(place)
    for k, ref in enumerate(refs[:-1]):
        out[:, lanes(q ^ k, FEAT)] = ref[...].astype(F32).T


def finish_kernel(rows, depth, outer, place, *refs):
    p, refs = refs[:4], refs[4:]
    pairs, (own_grown, other_grown, own_rest, other_rest, *outs, rest) = refs[:6], refs[6:]
    att, val_part, key_part = (
        [*(first.at[j] for j in range(3)), last.at[0]] for first, last in zip(pairs[:3], pairs[3:])
    )
    q, _, core = seat(place)
    for flip, ref in ((0, own_rest), (1, other_rest)):
        rest[pl.ds(pl.multiple_of((core ^ flip) * HALF, HALF), HALF), :] = ref[...].astype(F32)
    base = rest[...]
    own = [own_grown[j].astype(F32) for j in range(4)]
    other = [other_grown[j].astype(F32) for j in range(4)]
    for j, out in enumerate(outs):
        here = (q ^ j) * CORES + core
        later = base
        for i in range(4):
            for flip, group in ((0, own), (1, other)):
                if flip == 0 and i == j:
                    continue
                later = later + before(here, (q ^ i) * CORES + (core ^ flip)) * group[i]
        high, low = split(later)
        raw = p[j][depth : depth + rows, :]
        keys = jnp.maximum(raw, 0)
        vals = p[j][depth + rows :, :HEAD_DIM]
        d_val = val_part[j][...] + dot(keys, high) + dot(keys, low)
        d_key = key_part[j][...] + dot(vals, high, ((1,), (1,))) + dot(vals, low, ((1,), (1,)))
        out[:, :HEAD_DIM] = att[j][...]
        out[:, HEAD_DIM : 2 * HEAD_DIM] = d_val.astype(BF16)
        out[:, 2 * HEAD_DIM :] = jnp.where(raw.astype(F32) > 0, d_key, 0.0).astype(BF16)


def place_kernel(place, *refs):
    att, key_grad, val_grad = refs[-3:]
    q, _, _ = seat(place)
    for k, ref in enumerate(refs[:-3]):
        head = q ^ k
        att[:, lanes(head, HEAD_DIM)] = ref[:, :HEAD_DIM]
        val_grad[:, lanes(head, HEAD_DIM)] = ref[:, HEAD_DIM : 2 * HEAD_DIM]
        key_grad[:, lanes(head, FEAT)] = ref[:, 2 * HEAD_DIM :]


def body(hidden, w_query, key_input, values, cotangent):
    count = lax.axis_size("ctx")
    me = lax.axis_index("ctx")
    inner = CORES * HEADS_GROUP
    outer = count // inner
    rows, depth = key_input.shape[0], w_query.shape[0]
    if lax.axis_size("heads") > 1:
        hidden = lax.all_gather(hidden, "heads", axis=1, tiled=True)
    width = hidden.shape[1]
    place = me.astype(jnp.int32).reshape(1)

    def swap(block, bits):
        return lax.ppermute(block, "ctx", [(i, i ^ bits) for i in range(count)])

    def core_swap(block):
        return swap(block, 1)

    def chip_swap(block, k):
        return swap(block, CORES * k)

    def plane_swap(block, k):
        return swap(block, inner * k)

    packs = call(
        pack_kernel,
        [((depth + 2 * rows, FEAT), BF16)] * 4,
        [place, w_query, key_input, values, cotangent],
        scratch=[pltpu.SemaphoreType.DMA((16,))],
        space=pltpu.HBM,
        mib=59,
    )
    hidden, packs = lax.optimization_barrier((hidden, packs))
    p = [packs[0]] + [chip_swap(packs[k], k) for k in (1, 2, 3)]
    h1, h2 = chip_swap(hidden, 1), chip_swap(hidden, 2)
    start = call(
        functools.partial(own_kernel, rows, depth),
        [((depth, FEAT), BF16), ((FEAT, HEAD_DIM), F32)],
        [place, p[0]],
    )
    pay, states = call(
        functools.partial(state_kernel, rows, depth),
        [((4 * depth + HALF, FEAT), BF16), ((4, FEAT, HEAD_DIM), BF16)],
        [place, *start, *p[1:]],
        urgent=URGENT,
    )
    pays = [pay] + [None] * (outer - 1)
    for k in sorted(range(1, outer), key=lambda k: (k.bit_count(), -k)):
        pays[k] = plane_swap(pays[k & k - 1], k & -k)
    h1, h2, late_pay, late_states = lax.optimization_barrier((h1, h2, pay, states))
    h3 = [chip_swap(h1[: rows // 2], 2), chip_swap(h2[rows // 2 :], 1)]
    h = [hidden, h1, h2, *h3]
    other_pays = [core_swap(late_pay)] + [core_swap(pays[k]) for k in range(1, outer)]
    other_states = core_swap(late_states)
    positions = 4 * rows

    def kept(blocks):
        return [
            ((blocks, rows, HEAD_DIM), BF16),
            ((FEAT, blocks * rows), BF16),
            ((blocks, FEAT, HEAD_DIM), BF16),
            ((blocks, rows, FEAT), BF16),
            ((blocks, rows, HEAD_DIM), BF16),
            ((blocks, rows, rows), BF16),
            ((blocks, rows, rows), BF16),
        ]

    def side(parts):
        blocks = parts[0].shape[0]
        return call(
            side_kernel,
            [((blocks, rows, HEAD_DIM), F32), ((blocks, rows, FEAT), F32)],
            [place, *parts],
            flops=6 * blocks * rows * FEAT * HEAD_DIM,
        )

    *first, weights, high, low = call(
        functools.partial(attend_kernel, rows, depth, outer),
        kept(3) + [((width, FEAT), BF16), ((FEAT, HEAD_DIM), BF16), ((FEAT, HEAD_DIM), BF16)],
        [place, hidden, h1, h2, *p[:3], *pays, *other_pays, states, other_states],
        flops=2 * 3 * rows * width * FEAT,
        scratch=[pltpu.VMEM((3 * rows, FEAT), F32)],
    )
    *last, grown = call(
        functools.partial(last_kernel, rows, depth),
        kept(1) + [((4, FEAT, HEAD_DIM), BF16)],
        [place, *h3, weights, p[3], high, low, first[2]],
        flops=2 * rows * width * FEAT,
    )
    other_grown = core_swap(grown)
    sums = [None] * outer
    order = sorted(range(outer), key=lambda k: (-k.bit_count(), k))
    for k in order:
        keep, give = call(
            functools.partial(grad_kernel, depth, k),
            [((FEAT, 4 * depth), F32), ((FEAT, 4 * depth), BF16)],
            [place, *h, first[1], last[1]],
            flops=2 * positions * width * FEAT // outer,
        )
        gift = core_swap(give)
        if k == order[0]:
            extra = HALF * HEAD_DIM // (4 * depth)
            sums[k], half = call(
                functools.partial(load_kernel, depth),
                [((FEAT + extra, 4 * depth), BF16), ((HALF, HEAD_DIM), BF16)],
                [place, keep, gift, grown, other_grown],
                scratch=[pltpu.VMEM((FEAT, HEAD_DIM), F32)],
            )
        else:
            sums[k] = keep + gift.astype(F32)
    arrived, steps = [], []
    for k in order[:-1]:
        came, onward = plane_swap(sums[k].astype(BF16), k & -k), k & k - 1
        if k == order[0]:
            came, _ = lax.optimization_barrier((came, sums[order[1]].astype(BF16)))
            near, window = call(
                unload_kernel, [((HALF, HEAD_DIM), BF16)] * 2, [place, came, half]
            )
            steps.append(near)
            came = came[:FEAT]
        if onward:
            sums[onward] = sums[onward] + came.astype(F32)
        else:
            arrived.append(came)
    while 1 << len(steps) < outer:
        came = plane_swap(window, 1 << len(steps))
        steps.append(came)
        window = (window.astype(F32) + came.astype(F32)).astype(BF16)
    (rest,) = call(rest_kernel, [((HALF, HEAD_DIM), BF16)], [place, *steps])
    own = sums[0]
    other_rest = core_swap(rest)
    outs = call(
        functools.partial(finish_kernel, rows, depth, outer),
        [((rows, 2 * HEAD_DIM + FEAT), BF16)] * 4,
        [
            place,
            *p,
            *(first[0], *side(first[3:])),
            *(last[0], *side(last[3:])),
            grown,
            other_grown,
            rest,
            other_rest,
        ],
        flops=16 * positions * FEAT * HEAD_DIM,
        scratch=[pltpu.VMEM((FEAT, HEAD_DIM), F32)],
    )
    placed = [outs[0]] + [chip_swap(outs[k], k) for k in (1, 2, 3)]
    attended, key_grad, value_grad = call(
        place_kernel,
        [
            ((rows, HEADS_GROUP * HEAD_DIM), BF16),
            ((rows, HEADS_GROUP * FEAT), BF16),
            ((rows, HEADS_GROUP * HEAD_DIM), BF16),
        ],
        [place, *placed],
    )
    blocks = call(
        functools.partial(sum_kernel, depth),
        [((FEAT, depth), F32)] + [((FEAT, depth), BF16)] * 3,
        [place, own, *arrived],
        scratch=[pltpu.VMEM((4, FEAT, depth), F32)],
        urgent=URGENT,
    )
    columns = [blocks[0]] + [chip_swap(blocks[k], k) for k in (1, 2, 3)]
    (query_grad,) = call(
        query_grad_kernel, [((depth, HEADS_GROUP * FEAT), F32)], [place, *columns]
    )
    return (attended, query_grad, key_grad, value_grad)


def solution(mesh):
    return jax.shard_map(
        body,
        mesh=mesh,
        in_specs=(P("ctx", "heads"),) * 5,
        out_specs=(P("ctx", "heads"),) * 4,
        check_vma=False,
    )
```

```python
import functools

import jax
import jax.numpy as jnp
from jax import lax
from jax.experimental import pallas as pl
from jax.experimental.pallas import tpu as pltpu
from jax.sharding import PartitionSpec as P

HEAD_DIM = 128
FEAT = 256
HEADS_GROUP = 4
CORES = 2
EPSILON = 1e-06

F32 = jnp.float32
BF16 = jnp.bfloat16
HALF = FEAT // 2
URGENT = 1 << 35
HOPS = (3, 2, 1, 0)


def dot(a, b, dims=((1,), (0,))):
    return lax.dot_general(a, b, (dims, ((), ())), preferred_element_type=F32)


def split(x):
    high = x.astype(BF16)
    return high, (x - high.astype(F32)).astype(BF16)


def seat(place):
    me = place[0]
    low, high = CORES.bit_length() - 1, (CORES * HEADS_GROUP).bit_length() - 1
    return me >> low & HEADS_GROUP - 1, me >> high, me & CORES - 1


def call(kernel, outs, args, flops=0, scratch=(), mib=16, space=pltpu.VMEM, urgent=0):
    shapes = [jax.ShapeDtypeStruct(shape, dtype) for shape, dtype in outs]
    moved = sum(a.size * a.dtype.itemsize for a in args) + sum(s.size * s.dtype.itemsize for s in shapes)
    return pl.pallas_call(
        kernel,
        out_shape=shapes,
        in_specs=[pl.BlockSpec(memory_space=pltpu.SMEM)]
        + [pl.BlockSpec(memory_space=space)] * (len(args) - 1),
        out_specs=[pl.BlockSpec(memory_space=pltpu.VMEM)] * len(shapes),
        scratch_shapes=list(scratch),
        compiler_params=pltpu.CompilerParams(vmem_limit_bytes=mib << 20),
        cost_estimate=pl.CostEstimate(flops=urgent or flops, bytes_accessed=moved, transcendentals=0),
    )(*args)


def lanes(index, width):
    return pl.ds(pl.multiple_of(index * width, width), width)


def pack_kernel(place, w, key, val, cot, *refs):
    outs, sems = refs[:4], refs[4]
    rows, depth = key.shape[0], w.shape[0]
    q, _, _ = seat(place)
    copies = []
    for k in (3, 1, 2, 0):
        head, out = q ^ k, outs[k]
        low, high = pl.ds(depth, rows), pl.ds(depth + rows, rows)
        moves = (
            (w.at[:, lanes(head, FEAT)], out.at[pl.ds(0, depth), :]),
            (key.at[:, lanes(head, FEAT)], out.at[low, :]),
            (val.at[:, lanes(head, HEAD_DIM)], out.at[high, pl.ds(0, HEAD_DIM)]),
            (cot.at[:, lanes(head, HEAD_DIM)], out.at[high, pl.ds(HEAD_DIM, HEAD_DIM)]),
        )
        for source, target in moves:
            copies.append(pltpu.make_async_copy(source, target, sems.at[len(copies)]))
            copies[-1].start()
    for copy in copies:
        copy.wait()


def state_of(p, rows, depth):
    keys = jnp.maximum(p[depth : depth + rows, :], 0)
    return dot(keys, p[depth + rows :, :HEAD_DIM], ((0,), (0,)))


def own_kernel(rows, depth, place, p, shard, state):
    shard[...] = p[:depth, :]
    state[...] = state_of(p, rows, depth)


def state_kernel(rows, depth, place, shard, own_state, p3, p2, p1, pay, states):
    pay[:depth, :] = shard[...]
    total = own_state[...]
    states[0] = total.astype(BF16)
    for j, p in ((1, p1), (2, p2), (3, p3)):
        pay[j * depth : (j + 1) * depth, :] = p[:depth, :]
        state = state_of(p, rows, depth)
        states[j] = state.astype(BF16)
        total = total + state
    total = total.astype(BF16)
    pay[4 * depth :, :HEAD_DIM] = total[:HALF, :]
    pay[4 * depth :, HEAD_DIM:] = total[HALF:, :]


def hidden_columns(h, start, width):
    cols = pl.ds(start, width)
    return jnp.concatenate([ref[:, cols] for ref in h], axis=0)


def before(there, here):
    return (there < here).astype(jnp.int32).astype(F32)


def causal_mask(rows):
    return lax.broadcasted_iota(jnp.int32, (rows, rows), 0) >= lax.broadcasted_iota(
        jnp.int32, (rows, rows), 1
    )


def attend_block(j, rows, depth, query, p, prior_high, prior_low, outs):
    att, dq_t, grown, feats_out, d_num_out, scores_out, mixed_out = outs
    causal = causal_mask(rows)
    feats = jnp.maximum(query, 0.0).astype(BF16)
    keys = jnp.maximum(p[depth : depth + rows, :], 0)
    vals = p[depth + rows :, :HEAD_DIM]
    grad = p[depth + rows :, HEAD_DIM:].astype(F32)
    scores = jnp.where(causal, dot(feats, keys, ((1,), (1,))), 0.0).astype(BF16)
    numer = dot(scores, vals) + dot(feats, prior_high) + dot(feats, prior_low)
    inv = lax.rsqrt(jnp.mean(numer * numer, axis=-1, keepdims=True) + EPSILON)
    normed = numer * inv
    att[j] = normed.astype(BF16)
    d_num = (inv * (grad - normed * jnp.mean(grad * normed, axis=-1, keepdims=True))).astype(BF16)
    mixed = jnp.where(causal, dot(d_num, vals, ((1,), (1,))), 0.0).astype(BF16)
    d_feat = dot(mixed, keys) + dot(d_num, prior_high, ((1,), (1,))) + dot(d_num, prior_low, ((1,), (1,)))
    d_query = jnp.where(query > 0, d_feat, 0.0)
    dq_t[:, j * rows : (j + 1) * rows] = d_query.T.astype(BF16)
    grown[j] = dot(feats, d_num, ((0,), (0,))).astype(BF16)
    feats_out[j] = feats
    d_num_out[j] = d_num
    scores_out[j] = scores
    mixed_out[j] = mixed


def attend_kernel(rows, depth, outer, place, *refs):
    h, refs = refs[:3], refs[3:]
    p, refs = refs[:3], refs[3:]
    own_pay, refs = refs[:outer], refs[outer:]
    other_pay, refs = refs[:outer], refs[outer:]
    own_states, other_states, *outs, weights, last_high, last_low, proj = refs
    q, z, core = seat(place)
    base = jnp.zeros((FEAT, HEAD_DIM), F32)
    for k in range(outer):
        for flip, pay in ((0, own_pay[k]), (1, other_pay[k])):
            for j in range(4):
                at = (((z ^ k) * 4 + (q ^ j)) * CORES + (core ^ flip)) * depth
                weights[pl.ds(pl.multiple_of(at, depth), depth), :] = pay[j * depth : (j + 1) * depth, :]
            if k:
                packed = pay[4 * depth :, :].astype(F32)
                base = base + before(z ^ k, z) * jnp.concatenate(
                    [packed[:, :HEAD_DIM], packed[:, HEAD_DIM:]], axis=0
                )
    width = h[0].shape[1]
    step = min(512, width)
    for at in range(0, width, step):
        part = dot(hidden_columns(h, at, step), weights[at : at + step, :])
        if at:
            proj[...] += part
        else:
            proj[...] = part
    own = [own_states[j].astype(F32) for j in range(4)]
    other = [other_states[j].astype(F32) for j in range(4)]
    for j in range(4):
        here = (q ^ j) * CORES + core
        prior = base
        for i in range(4):
            for flip, group in ((0, own), (1, other)):
                if flip == 0 and i == j:
                    continue
                prior = prior + before((q ^ i) * CORES + (core ^ flip), here) * group[i]
        high, low = split(prior)
        if j < 3:
            attend_block(j, rows, depth, proj[j * rows : (j + 1) * rows, :], p[j], high, low, outs)
        else:
            last_high[...] = high
            last_low[...] = low


def last_kernel(rows, depth, place, top, bottom, weights, p, high, low, grown, *outs):
    *outs, every = outs
    query = dot(jnp.concatenate([top[...], bottom[...]], axis=0), weights[...])
    attend_block(0, rows, depth, query, p, high[...], low[...], outs)
    every[:3] = grown[...]
    every[3] = outs[2][0]


def load_kernel(depth, place, keep, gift, *refs):
    *parts, load, half, total = refs
    _, _, core = seat(place)
    load[:FEAT, :] = (keep[...] + gift[...].astype(F32)).astype(BF16)
    total[...] = sum(ref[j].astype(F32) for ref in parts for j in range(ref.shape[0]))
    mine = total[pl.ds(pl.multiple_of(core * HALF, HALF), HALF), :].astype(BF16)
    half[...] = mine
    wide = load.shape[1] // HEAD_DIM
    tall = HALF // wide
    for i in range(wide):
        load[FEAT:, i * HEAD_DIM : (i + 1) * HEAD_DIM] = mine[i * tall : (i + 1) * tall, :]


def unload_kernel(place, load, half, came, window):
    wide = load.shape[1] // HEAD_DIM
    tall = HALF // wide
    for i in range(wide):
        came[i * tall : (i + 1) * tall, :] = load[FEAT:, i * HEAD_DIM : (i + 1) * HEAD_DIM]
    window[...] = (half[...].astype(F32) + came[...].astype(F32)).astype(BF16)


def rest_kernel(place, *refs):
    *steps, rest = refs
    _, z, _ = seat(place)
    total = jnp.zeros(rest.shape, F32)
    for i, ref in enumerate(steps):
        total = total + before(z, z ^ 1 << i) * ref[...].astype(F32)
    rest[...] = total.astype(BF16)


def side_kernel(place, feats, d_num, scores, mixed, val_part, key_part):
    for j in range(feats.shape[0]):
        val_part[j] = dot(scores[j], d_num[j], ((0,), (0,)))
        key_part[j] = dot(mixed[j], feats[j], ((0,), (0,)))


def grad_kernel(depth, k, place, *refs):
    *h, dq_first, dq_last, keep, give = refs
    _, z, core = seat(place)
    pair = CORES * depth
    lhs = jnp.concatenate([dq_first[...], dq_last[...]], axis=1)
    for i in range(4):
        start = pl.multiple_of(((z ^ k) * 4 + i) * pair, pair)
        out = dot(lhs, hidden_columns(h, start, pair))
        even, odd = out[:, :depth], out[:, depth:]
        first = jnp.broadcast_to(core == 0, even.shape)
        keep[:, i * depth : (i + 1) * depth] = jnp.where(first, even, odd)
        give[:, i * depth : (i + 1) * depth] = jnp.where(first, odd, even).astype(BF16)


def sum_kernel(depth, place, own, *refs):
    arrived, (mine, *outs), blocks = refs[:-5], refs[-5:-1], refs[-1]
    total = own[...]
    for ref in arrived:
        total = total + ref[...].astype(F32)
    q, _, _ = seat(place)
    for i in range(4):
        blocks[q ^ i] = total[:, i * depth : (i + 1) * depth]
    mine[...] = blocks[0]
    for k, out in enumerate(outs):
        out[...] = blocks[k + 1].astype(BF16)


def query_grad_kernel(place, *refs):
    out = refs[-1]
    q, _, _ = seat(place)
    for k, ref in zip(HOPS, refs[:-1]):
        out[:, lanes(q ^ k, FEAT)] = ref[...].astype(F32).T


def finish_kernel(rows, depth, outer, place, *refs):
    p, refs = refs[:4], refs[4:]
    pairs, (own_grown, other_grown, own_rest, other_rest, *outs, rest) = refs[:6], refs[6:]
    att, val_part, key_part = (
        [*(first.at[j] for j in range(3)), last.at[0]] for first, last in zip(pairs[:3], pairs[3:])
    )
    q, _, core = seat(place)
    for flip, ref in ((0, own_rest), (1, other_rest)):
        rest[pl.ds(pl.multiple_of((core ^ flip) * HALF, HALF), HALF), :] = ref[...].astype(F32)
    base = rest[...]
    own = [own_grown[j].astype(F32) for j in range(4)]
    other = [other_grown[j].astype(F32) for j in range(4)]
    for j, out in enumerate(outs):
        here = (q ^ j) * CORES + core
        later = base
        for i in range(4):
            for flip, group in ((0, own), (1, other)):
                if flip == 0 and i == j:
                    continue
                later = later + before(here, (q ^ i) * CORES + (core ^ flip)) * group[i]
        high, low = split(later)
        raw = p[j][depth : depth + rows, :]
        keys = jnp.maximum(raw, 0)
        vals = p[j][depth + rows :, :HEAD_DIM]
        d_val = val_part[j][...] + dot(keys, high) + dot(keys, low)
        d_key = key_part[j][...] + dot(vals, high, ((1,), (1,))) + dot(vals, low, ((1,), (1,)))
        out[:, :HEAD_DIM] = att[j][...]
        out[:, HEAD_DIM : 2 * HEAD_DIM] = d_val.astype(BF16)
        out[:, 2 * HEAD_DIM :] = jnp.where(raw.astype(F32) > 0, d_key, 0.0).astype(BF16)


def place_kernel(place, *refs):
    att, key_grad, val_grad = refs[-3:]
    q, _, _ = seat(place)
    for k, ref in zip(HOPS, refs[:-3]):
        head = q ^ k
        att[:, lanes(head, HEAD_DIM)] = ref[:, :HEAD_DIM]
        val_grad[:, lanes(head, HEAD_DIM)] = ref[:, HEAD_DIM : 2 * HEAD_DIM]
        key_grad[:, lanes(head, FEAT)] = ref[:, 2 * HEAD_DIM :]


def body(hidden, w_query, key_input, values, cotangent):
    count = lax.axis_size("ctx")
    me = lax.axis_index("ctx")
    inner = CORES * HEADS_GROUP
    outer = count // inner
    rows, depth = key_input.shape[0], w_query.shape[0]
    if lax.axis_size("heads") > 1:
        hidden = lax.all_gather(hidden, "heads", axis=1, tiled=True)
    width = hidden.shape[1]
    place = me.astype(jnp.int32).reshape(1)

    def swap(block, bits):
        return lax.ppermute(block, "ctx", [(i, i ^ bits) for i in range(count)])

    def core_swap(block):
        return swap(block, 1)

    def chip_swap(block, k):
        return swap(block, CORES * k)

    def plane_swap(block, k):
        return swap(block, inner * k)

    packs = call(
        pack_kernel,
        [((depth + 2 * rows, FEAT), BF16)] * 4,
        [place, w_query, key_input, values, cotangent],
        scratch=[pltpu.SemaphoreType.DMA((16,))],
        space=pltpu.HBM,
        mib=59,
    )
    hidden, packs = lax.optimization_barrier((hidden, packs))
    p = [packs[0]] + [chip_swap(packs[k], k) for k in (1, 2, 3)]
    h1, h2 = chip_swap(hidden, 1), chip_swap(hidden, 2)
    start = call(
        functools.partial(own_kernel, rows, depth),
        [((depth, FEAT), BF16), ((FEAT, HEAD_DIM), F32)],
        [place, p[0]],
    )
    pay, states = call(
        functools.partial(state_kernel, rows, depth),
        [((4 * depth + HALF, FEAT), BF16), ((4, FEAT, HEAD_DIM), BF16)],
        [place, *start, *(p[k] for k in HOPS[:3])],
        urgent=URGENT,
    )
    pays = [pay] + [None] * (outer - 1)
    for k in sorted(range(1, outer), key=lambda k: (k.bit_count(), -k)):
        pays[k] = plane_swap(pays[k & k - 1], k & -k)
    h1, h2, late_pay, late_states = lax.optimization_barrier((h1, h2, pay, states))
    h3 = [chip_swap(h1[: rows // 2], 2), chip_swap(h2[rows // 2 :], 1)]
    h = [hidden, h1, h2, *h3]
    other_pays = [core_swap(late_pay)] + [core_swap(pays[k]) for k in range(1, outer)]
    other_states = core_swap(late_states)
    positions = 4 * rows

    def kept(blocks):
        return [
            ((blocks, rows, HEAD_DIM), BF16),
            ((FEAT, blocks * rows), BF16),
            ((blocks, FEAT, HEAD_DIM), BF16),
            ((blocks, rows, FEAT), BF16),
            ((blocks, rows, HEAD_DIM), BF16),
            ((blocks, rows, rows), BF16),
            ((blocks, rows, rows), BF16),
        ]

    def side(parts):
        blocks = parts[0].shape[0]
        return call(
            side_kernel,
            [((blocks, rows, HEAD_DIM), F32), ((blocks, rows, FEAT), F32)],
            [place, *parts],
            flops=6 * blocks * rows * FEAT * HEAD_DIM,
        )

    *first, weights, high, low = call(
        functools.partial(attend_kernel, rows, depth, outer),
        kept(3) + [((width, FEAT), BF16), ((FEAT, HEAD_DIM), BF16), ((FEAT, HEAD_DIM), BF16)],
        [place, hidden, h1, h2, *p[:3], *pays, *other_pays, states, other_states],
        flops=2 * 3 * rows * width * FEAT,
        scratch=[pltpu.VMEM((3 * rows, FEAT), F32)],
    )
    *last, grown = call(
        functools.partial(last_kernel, rows, depth),
        kept(1) + [((4, FEAT, HEAD_DIM), BF16)],
        [place, *h3, weights, p[3], high, low, first[2]],
        flops=2 * rows * width * FEAT,
    )
    other_grown = core_swap(grown)
    sums = [None] * outer
    order = sorted(range(outer), key=lambda k: (-k.bit_count(), k))
    for k in order:
        keep, give = call(
            functools.partial(grad_kernel, depth, k),
            [((FEAT, 4 * depth), F32), ((FEAT, 4 * depth), BF16)],
            [place, *h, first[1], last[1]],
            flops=2 * positions * width * FEAT // outer,
        )
        gift = core_swap(give)
        if k == order[0]:
            extra = HALF * HEAD_DIM // (4 * depth)
            sums[k], half = call(
                functools.partial(load_kernel, depth),
                [((FEAT + extra, 4 * depth), BF16), ((HALF, HEAD_DIM), BF16)],
                [place, keep, gift, grown, other_grown],
                scratch=[pltpu.VMEM((FEAT, HEAD_DIM), F32)],
            )
        else:
            sums[k] = keep + gift.astype(F32)
    arrived, steps = [], []
    for k in order[:-1]:
        came, onward = plane_swap(sums[k].astype(BF16), k & -k), k & k - 1
        if k == order[0]:
            came, _ = lax.optimization_barrier((came, sums[order[1]].astype(BF16)))
            near, window = call(
                unload_kernel, [((HALF, HEAD_DIM), BF16)] * 2, [place, came, half]
            )
            steps.append(near)
            came = came[:FEAT]
        if onward:
            sums[onward] = sums[onward] + came.astype(F32)
        else:
            arrived.append(came)
    while 1 << len(steps) < outer:
        came = plane_swap(window, 1 << len(steps))
        steps.append(came)
        window = (window.astype(F32) + came.astype(F32)).astype(BF16)
    (rest,) = call(rest_kernel, [((HALF, HEAD_DIM), BF16)], [place, *steps])
    own = sums[0]
    other_rest = core_swap(rest)
    outs = call(
        functools.partial(finish_kernel, rows, depth, outer),
        [((rows, 2 * HEAD_DIM + FEAT), BF16)] * 4,
        [
            place,
            *p,
            *(first[0], *side(first[3:])),
            *(last[0], *side(last[3:])),
            grown,
            other_grown,
            rest,
            other_rest,
        ],
        flops=16 * positions * FEAT * HEAD_DIM,
        scratch=[pltpu.VMEM((FEAT, HEAD_DIM), F32)],
    )
    placed = [outs[0]] + [chip_swap(outs[k], k) for k in (1, 2, 3)]
    attended, key_grad, value_grad = call(
        place_kernel,
        [
            ((rows, HEADS_GROUP * HEAD_DIM), BF16),
            ((rows, HEADS_GROUP * FEAT), BF16),
            ((rows, HEADS_GROUP * HEAD_DIM), BF16),
        ],
        [place, *(placed[k] for k in HOPS)],
    )
    blocks = call(
        functools.partial(sum_kernel, depth),
        [((FEAT, depth), F32)] + [((FEAT, depth), BF16)] * 3,
        [place, own, *arrived],
        scratch=[pltpu.VMEM((4, FEAT, depth), F32)],
        urgent=URGENT,
    )
    columns = [blocks[0]] + [chip_swap(blocks[k], k) for k in (1, 2, 3)]
    (query_grad,) = call(
        query_grad_kernel, [((depth, HEADS_GROUP * FEAT), F32)], [place, *(columns[k] for k in HOPS)]
    )
    return (attended, query_grad, key_grad, value_grad)


def solution(mesh):
    return jax.shard_map(
        body,
        mesh=mesh,
        in_specs=(P("ctx", "heads"),) * 5,
        out_specs=(P("ctx", "heads"),) * 4,
        check_vma=False,
    )
```

```python
import functools

import jax
import jax.numpy as jnp
from jax import lax
from jax.experimental import pallas as pl
from jax.experimental.pallas import tpu as pltpu
from jax.sharding import PartitionSpec as P

HEAD_DIM = 128
FEAT = 256
HEADS_GROUP = 4
CORES = 2
EPSILON = 1e-06

F32 = jnp.float32
BF16 = jnp.bfloat16
HALF = FEAT // 2
URGENT = 1 << 35
HOPS = (3, 2, 1, 0)


def dot(a, b, dims=((1,), (0,))):
    return lax.dot_general(a, b, (dims, ((), ())), preferred_element_type=F32)


def split(x):
    high = x.astype(BF16)
    return high, (x - high.astype(F32)).astype(BF16)


def seat(place):
    me = place[0]
    low, high = CORES.bit_length() - 1, (CORES * HEADS_GROUP).bit_length() - 1
    return me >> low & HEADS_GROUP - 1, me >> high, me & CORES - 1


def call(kernel, outs, args, flops=0, scratch=(), mib=16, space=pltpu.VMEM, urgent=0):
    shapes = [jax.ShapeDtypeStruct(shape, dtype) for shape, dtype in outs]
    moved = sum(a.size * a.dtype.itemsize for a in args) + sum(s.size * s.dtype.itemsize for s in shapes)
    return pl.pallas_call(
        kernel,
        out_shape=shapes,
        in_specs=[pl.BlockSpec(memory_space=pltpu.SMEM)]
        + [pl.BlockSpec(memory_space=space)] * (len(args) - 1),
        out_specs=[pl.BlockSpec(memory_space=pltpu.VMEM)] * len(shapes),
        scratch_shapes=list(scratch),
        compiler_params=pltpu.CompilerParams(vmem_limit_bytes=mib << 20),
        cost_estimate=pl.CostEstimate(flops=urgent or flops, bytes_accessed=moved, transcendentals=0),
    )(*args)


def lanes(index, width):
    return pl.ds(pl.multiple_of(index * width, width), width)


def pack_kernel(place, w, key, val, cot, *refs):
    outs, sems = refs[:4], refs[4]
    rows, depth = key.shape[0], w.shape[0]
    q, _, _ = seat(place)
    copies = []
    for k in (3, 1, 2, 0):
        head, out = q ^ k, outs[k]
        low, high = pl.ds(depth, rows), pl.ds(depth + rows, rows)
        moves = (
            (w.at[:, lanes(head, FEAT)], out.at[pl.ds(0, depth), :]),
            (key.at[:, lanes(head, FEAT)], out.at[low, :]),
            (val.at[:, lanes(head, HEAD_DIM)], out.at[high, pl.ds(0, HEAD_DIM)]),
            (cot.at[:, lanes(head, HEAD_DIM)], out.at[high, pl.ds(HEAD_DIM, HEAD_DIM)]),
        )
        for source, target in moves:
            copies.append(pltpu.make_async_copy(source, target, sems.at[len(copies)]))
            copies[-1].start()
    for copy in copies:
        copy.wait()


def state_of(p, rows, depth):
    keys = jnp.maximum(p[depth : depth + rows, :], 0)
    return dot(keys, p[depth + rows :, :HEAD_DIM], ((0,), (0,)))


def own_kernel(rows, depth, place, p, shard, state):
    shard[...] = p[:depth, :]
    state[...] = state_of(p, rows, depth)


def state_kernel(rows, depth, place, shard, own_state, p3, p2, p1, pay, states):
    pay[:depth, :] = shard[...]
    total = own_state[...]
    states[0] = total.astype(BF16)
    for j, p in ((1, p1), (2, p2), (3, p3)):
        pay[j * depth : (j + 1) * depth, :] = p[:depth, :]
        state = state_of(p, rows, depth)
        states[j] = state.astype(BF16)
        total = total + state
    total = total.astype(BF16)
    pay[4 * depth :, :HEAD_DIM] = total[:HALF, :]
    pay[4 * depth :, HEAD_DIM:] = total[HALF:, :]


def hidden_columns(h, start, width):
    cols = pl.ds(start, width)
    return jnp.concatenate([ref[:, cols] for ref in h], axis=0)


def before(there, here):
    return (there < here).astype(jnp.int32).astype(F32)


def causal_mask(rows):
    return lax.broadcasted_iota(jnp.int32, (rows, rows), 0) >= lax.broadcasted_iota(
        jnp.int32, (rows, rows), 1
    )


def attend_block(j, rows, depth, query, p, prior_high, prior_low, outs):
    att, dq_t, grown, feats_out, d_num_out, scores_out, mixed_out = outs
    causal = causal_mask(rows)
    feats = jnp.maximum(query, 0.0).astype(BF16)
    keys = jnp.maximum(p[depth : depth + rows, :], 0)
    vals = p[depth + rows :, :HEAD_DIM]
    grad = p[depth + rows :, HEAD_DIM:].astype(F32)
    scores = jnp.where(causal, dot(feats, keys, ((1,), (1,))), 0.0).astype(BF16)
    numer = dot(scores, vals) + dot(feats, prior_high) + dot(feats, prior_low)
    inv = lax.rsqrt(jnp.mean(numer * numer, axis=-1, keepdims=True) + EPSILON)
    normed = numer * inv
    att[j] = normed.astype(BF16)
    d_num = (inv * (grad - normed * jnp.mean(grad * normed, axis=-1, keepdims=True))).astype(BF16)
    mixed = jnp.where(causal, dot(d_num, vals, ((1,), (1,))), 0.0).astype(BF16)
    d_feat = dot(mixed, keys) + dot(d_num, prior_high, ((1,), (1,))) + dot(d_num, prior_low, ((1,), (1,)))
    d_query = jnp.where(query > 0, d_feat, 0.0)
    dq_t[:, j * rows : (j + 1) * rows] = d_query.T.astype(BF16)
    grown[j] = dot(feats, d_num, ((0,), (0,))).astype(BF16)
    feats_out[j] = feats
    d_num_out[j] = d_num
    scores_out[j] = scores
    mixed_out[j] = mixed


def attend_kernel(rows, depth, outer, place, *refs):
    h, refs = refs[:3], refs[3:]
    p, refs = refs[:3], refs[3:]
    own_pay, refs = refs[:outer], refs[outer:]
    other_pay, refs = refs[:outer], refs[outer:]
    own_states, other_states, *outs, weights, last_high, last_low, proj = refs
    q, z, core = seat(place)
    base = jnp.zeros((FEAT, HEAD_DIM), F32)
    for k in range(outer):
        for flip, pay in ((0, own_pay[k]), (1, other_pay[k])):
            for j in range(4):
                at = (((z ^ k) * 4 + (q ^ j)) * CORES + (core ^ flip)) * depth
                weights[pl.ds(pl.multiple_of(at, depth), depth), :] = pay[j * depth : (j + 1) * depth, :]
            if k:
                packed = pay[4 * depth :, :].astype(F32)
                base = base + before(z ^ k, z) * jnp.concatenate(
                    [packed[:, :HEAD_DIM], packed[:, HEAD_DIM:]], axis=0
                )
    width = h[0].shape[1]
    step = min(512, width)
    for at in range(0, width, step):
        part = dot(hidden_columns(h, at, step), weights[at : at + step, :])
        if at:
            proj[...] += part
        else:
            proj[...] = part
    own = [own_states[j].astype(F32) for j in range(4)]
    other = [other_states[j].astype(F32) for j in range(4)]
    for j in range(4):
        here = (q ^ j) * CORES + core
        prior = base
        for i in range(4):
            for flip, group in ((0, own), (1, other)):
                if flip == 0 and i == j:
                    continue
                prior = prior + before((q ^ i) * CORES + (core ^ flip), here) * group[i]
        high, low = split(prior)
        if j < 3:
            attend_block(j, rows, depth, proj[j * rows : (j + 1) * rows, :], p[j], high, low, outs)
        else:
            last_high[...] = high
            last_low[...] = low


def last_kernel(rows, depth, place, top, bottom, weights, p, high, low, grown, *outs):
    *outs, every = outs
    query = dot(jnp.concatenate([top[...], bottom[...]], axis=0), weights[...])
    attend_block(0, rows, depth, query, p, high[...], low[...], outs)
    every[:3] = grown[...]
    every[3] = outs[2][0]


def load_kernel(depth, place, keep, gift, *refs):
    *parts, load, half, total = refs
    _, _, core = seat(place)
    load[:FEAT, :] = (keep[...] + gift[...].astype(F32)).astype(BF16)
    total[...] = sum(ref[j].astype(F32) for ref in parts for j in range(ref.shape[0]))
    mine = total[pl.ds(pl.multiple_of(core * HALF, HALF), HALF), :].astype(BF16)
    half[...] = mine
    wide = load.shape[1] // HEAD_DIM
    tall = HALF // wide
    for i in range(wide):
        load[FEAT:, i * HEAD_DIM : (i + 1) * HEAD_DIM] = mine[i * tall : (i + 1) * tall, :]


def unload_kernel(place, load, half, came, window):
    wide = load.shape[1] // HEAD_DIM
    tall = HALF // wide
    for i in range(wide):
        came[i * tall : (i + 1) * tall, :] = load[FEAT:, i * HEAD_DIM : (i + 1) * HEAD_DIM]
    window[...] = (half[...].astype(F32) + came[...].astype(F32)).astype(BF16)


def rest_kernel(place, *refs):
    *steps, rest = refs
    _, z, _ = seat(place)
    total = jnp.zeros(rest.shape, F32)
    for i, ref in enumerate(steps):
        total = total + before(z, z ^ 1 << i) * ref[...].astype(F32)
    rest[...] = total.astype(BF16)


def side_kernel(place, feats, d_num, scores, mixed, val_part, key_part):
    for j in range(feats.shape[0]):
        val_part[j] = dot(scores[j], d_num[j], ((0,), (0,)))
        key_part[j] = dot(mixed[j], feats[j], ((0,), (0,)))


def grad_kernel(depth, k, place, *refs):
    *h, dq_first, dq_last, keep, give = refs
    _, z, core = seat(place)
    pair = CORES * depth
    lhs = jnp.concatenate([dq_first[...], dq_last[...]], axis=1)
    for i in range(4):
        start = pl.multiple_of(((z ^ k) * 4 + i) * pair, pair)
        out = dot(lhs, hidden_columns(h, start, pair))
        even, odd = out[:, :depth], out[:, depth:]
        first = jnp.broadcast_to(core == 0, even.shape)
        keep[:, i * depth : (i + 1) * depth] = jnp.where(first, even, odd)
        give[:, i * depth : (i + 1) * depth] = jnp.where(first, odd, even).astype(BF16)


def sum_kernel(depth, place, own, *refs):
    arrived, (mine, *outs), blocks = refs[:-5], refs[-5:-1], refs[-1]
    total = own[...]
    for ref in arrived:
        total = total + ref[...].astype(F32)
    q, _, _ = seat(place)
    for i in range(4):
        blocks[q ^ i] = total[:, i * depth : (i + 1) * depth]
    mine[...] = blocks[0]
    for k, out in enumerate(outs):
        out[...] = blocks[k + 1].astype(BF16)


def query_grad_kernel(place, *refs):
    out = refs[-1]
    q, _, _ = seat(place)
    for k, ref in zip(HOPS, refs[:-1]):
        out[:, lanes(q ^ k, FEAT)] = ref[...].astype(F32).T


def finish_kernel(rows, depth, outer, place, *refs):
    p, refs = refs[:4], refs[4:]
    pairs, (own_grown, other_grown, own_rest, other_rest, *outs, rest) = refs[:6], refs[6:]
    att, val_part, key_part = (
        [*(first.at[j] for j in range(3)), last.at[0]] for first, last in zip(pairs[:3], pairs[3:])
    )
    q, _, core = seat(place)
    for flip, ref in ((0, own_rest), (1, other_rest)):
        rest[pl.ds(pl.multiple_of((core ^ flip) * HALF, HALF), HALF), :] = ref[...].astype(F32)
    base = rest[...]
    own = [own_grown[j].astype(F32) for j in range(4)]
    other = [other_grown[j].astype(F32) for j in range(4)]
    for j, out in enumerate(outs):
        here = (q ^ j) * CORES + core
        later = base
        for i in range(4):
            for flip, group in ((0, own), (1, other)):
                if flip == 0 and i == j:
                    continue
                later = later + before(here, (q ^ i) * CORES + (core ^ flip)) * group[i]
        high, low = split(later)
        raw = p[j][depth : depth + rows, :]
        keys = jnp.maximum(raw, 0)
        vals = p[j][depth + rows :, :HEAD_DIM]
        d_val = val_part[j][...] + dot(keys, high) + dot(keys, low)
        d_key = key_part[j][...] + dot(vals, high, ((1,), (1,))) + dot(vals, low, ((1,), (1,)))
        out[:, :HEAD_DIM] = att[j][...]
        out[:, HEAD_DIM : 2 * HEAD_DIM] = d_val.astype(BF16)
        out[:, 2 * HEAD_DIM :] = jnp.where(raw.astype(F32) > 0, d_key, 0.0).astype(BF16)


def place_kernel(place, *refs):
    att, key_grad, val_grad = refs[-3:]
    q, _, _ = seat(place)
    for k, ref in zip(HOPS, refs[:-3]):
        head = q ^ k
        att[:, lanes(head, HEAD_DIM)] = ref[:, :HEAD_DIM]
        val_grad[:, lanes(head, HEAD_DIM)] = ref[:, HEAD_DIM : 2 * HEAD_DIM]
        key_grad[:, lanes(head, FEAT)] = ref[:, 2 * HEAD_DIM :]


def body(hidden, w_query, key_input, values, cotangent):
    count = lax.axis_size("ctx")
    me = lax.axis_index("ctx")
    inner = CORES * HEADS_GROUP
    outer = count // inner
    rows, depth = key_input.shape[0], w_query.shape[0]
    if lax.axis_size("heads") > 1:
        hidden = lax.all_gather(hidden, "heads", axis=1, tiled=True)
    width = hidden.shape[1]
    place = me.astype(jnp.int32).reshape(1)

    def swap(block, bits):
        return lax.ppermute(block, "ctx", [(i, i ^ bits) for i in range(count)])

    def core_swap(block):
        return swap(block, 1)

    def chip_swap(block, k):
        return swap(block, CORES * k)

    def plane_swap(block, k):
        return swap(block, inner * k)

    packs = call(
        pack_kernel,
        [((depth + 2 * rows, FEAT), BF16)] * 4,
        [place, w_query, key_input, values, cotangent],
        scratch=[pltpu.SemaphoreType.DMA((16,))],
        space=pltpu.HBM,
        mib=59,
    )
    hidden, packs = lax.optimization_barrier((hidden, packs))
    p = [packs[0]] + [chip_swap(packs[k], k) for k in (1, 2, 3)]
    h1, h2 = chip_swap(hidden, 1), chip_swap(hidden, 2)
    start = call(
        functools.partial(own_kernel, rows, depth),
        [((depth, FEAT), BF16), ((FEAT, HEAD_DIM), F32)],
        [place, p[0]],
    )
    pay, states = call(
        functools.partial(state_kernel, rows, depth),
        [((4 * depth + HALF, FEAT), BF16), ((4, FEAT, HEAD_DIM), BF16)],
        [place, *start, *(p[k] for k in HOPS[:3])],
        urgent=URGENT,
    )
    pays = [pay] + [None] * (outer - 1)
    for k in sorted(range(1, outer), key=lambda k: (k.bit_count(), -k)):
        pays[k] = plane_swap(pays[k & k - 1], k & -k)
    h1, h2, late_pay, late_states = lax.optimization_barrier((h1, h2, pay, states))
    h3 = [chip_swap(h1[: rows // 2], 2), chip_swap(h2[rows // 2 :], 1)]
    h = [hidden, h1, h2, *h3]
    other_pays = [core_swap(late_pay)] + [core_swap(pays[k]) for k in range(1, outer)]
    other_states = core_swap(late_states)
    positions = 4 * rows

    def kept(blocks):
        return [
            ((blocks, rows, HEAD_DIM), BF16),
            ((FEAT, blocks * rows), BF16),
            ((blocks, FEAT, HEAD_DIM), BF16),
            ((blocks, rows, FEAT), BF16),
            ((blocks, rows, HEAD_DIM), BF16),
            ((blocks, rows, rows), BF16),
            ((blocks, rows, rows), BF16),
        ]

    def side(parts):
        blocks = parts[0].shape[0]
        return call(
            side_kernel,
            [((blocks, rows, HEAD_DIM), F32), ((blocks, rows, FEAT), F32)],
            [place, *parts],
            flops=6 * blocks * rows * FEAT * HEAD_DIM,
        )

    *first, weights, high, low = call(
        functools.partial(attend_kernel, rows, depth, outer),
        kept(3) + [((width, FEAT), BF16), ((FEAT, HEAD_DIM), BF16), ((FEAT, HEAD_DIM), BF16)],
        [place, hidden, h1, h2, *p[:3], *pays, *other_pays, states, other_states],
        flops=2 * 3 * rows * width * FEAT,
        scratch=[pltpu.VMEM((3 * rows, FEAT), F32)],
    )
    *last, grown = call(
        functools.partial(last_kernel, rows, depth),
        kept(1) + [((4, FEAT, HEAD_DIM), BF16)],
        [place, *h3, weights, p[3], high, low, first[2]],
        flops=2 * rows * width * FEAT,
    )
    other_grown = core_swap(grown)
    sums = [None] * outer
    order = sorted(range(outer), key=lambda k: (-k.bit_count(), k))
    for k in order:
        keep, give = call(
            functools.partial(grad_kernel, depth, k),
            [((FEAT, 4 * depth), F32), ((FEAT, 4 * depth), BF16)],
            [place, *h, first[1], last[1]],
            flops=2 * positions * width * FEAT // outer,
        )
        gift = core_swap(give)
        if k == order[0]:
            extra = HALF * HEAD_DIM // (4 * depth)
            sums[k], half = call(
                functools.partial(load_kernel, depth),
                [((FEAT + extra, 4 * depth), BF16), ((HALF, HEAD_DIM), BF16)],
                [place, keep, gift, grown, other_grown],
                scratch=[pltpu.VMEM((FEAT, HEAD_DIM), F32)],
            )
        else:
            sums[k] = keep + gift.astype(F32)
    arrived, steps = [], []
    for k in order[:-1]:
        came, onward = plane_swap(sums[k].astype(BF16), k & -k), k & k - 1
        if k == order[0]:
            near, window = call(
                unload_kernel, [((HALF, HEAD_DIM), BF16)] * 2, [place, came, half]
            )
            steps.append(near)
            came = came[:FEAT]
        if onward:
            sums[onward] = sums[onward] + came.astype(F32)
        else:
            arrived.append(came)
    while 1 << len(steps) < outer:
        came = plane_swap(window, 1 << len(steps))
        steps.append(came)
        window = (window.astype(F32) + came.astype(F32)).astype(BF16)
    (rest,) = call(rest_kernel, [((HALF, HEAD_DIM), BF16)], [place, *steps])
    own = sums[0]
    other_rest = core_swap(rest)
    outs = call(
        functools.partial(finish_kernel, rows, depth, outer),
        [((rows, 2 * HEAD_DIM + FEAT), BF16)] * 4,
        [
            place,
            *p,
            *(first[0], *side(first[3:])),
            *(last[0], *side(last[3:])),
            grown,
            other_grown,
            rest,
            other_rest,
        ],
        flops=16 * positions * FEAT * HEAD_DIM,
        scratch=[pltpu.VMEM((FEAT, HEAD_DIM), F32)],
    )
    placed = [outs[0]] + [chip_swap(outs[k], k) for k in (1, 2, 3)]
    attended, key_grad, value_grad = call(
        place_kernel,
        [
            ((rows, HEADS_GROUP * HEAD_DIM), BF16),
            ((rows, HEADS_GROUP * FEAT), BF16),
            ((rows, HEADS_GROUP * HEAD_DIM), BF16),
        ],
        [place, *(placed[k] for k in HOPS)],
    )
    blocks = call(
        functools.partial(sum_kernel, depth),
        [((FEAT, depth), F32)] + [((FEAT, depth), BF16)] * 3,
        [place, own, *arrived],
        scratch=[pltpu.VMEM((4, FEAT, depth), F32)],
        urgent=URGENT,
    )
    columns = [blocks[0]] + [chip_swap(blocks[k], k) for k in (1, 2, 3)]
    (query_grad,) = call(
        query_grad_kernel, [((depth, HEADS_GROUP * FEAT), F32)], [place, *(columns[k] for k in HOPS)]
    )
    return (attended, query_grad, key_grad, value_grad)


def solution(mesh):
    return jax.shard_map(
        body,
        mesh=mesh,
        in_specs=(P("ctx", "heads"),) * 5,
        out_specs=(P("ctx", "heads"),) * 4,
        check_vma=False,
    )
```
